128 devices in a mesh: row: 16 (over x, z), col: 8 (over y, core).
Axes of the slice: x: 4, y: 4, z: 4, core: 2. Of those that a mesh axis runs over, the one named last changes fastest.
Arguments:
- tmatrix: bfloat16 [10656, 10656], P('row', 'col'), may hold values from -0.0625 to 0.0625
- panel: bfloat16 [10656, 2048], P('col', 'row'), may hold values from -6 to 6
- contrast: float32 [3, 144, 288], replicated, may hold values from -1.5 to 1.5
Outputs:
- excitation: bfloat16 [10656, 2048], P('col', 'row')
The draws below stay inside these ranges and needn't reach their ends.
All inputs are finite; a program needn't handle non-finite values.
Results may differ from the reference program's by a relative error of at most 0.006.
Values may be sent and summed in bfloat16 or wider, within the bound.
A program may use at most 128 MiB of HBM per device.

```python
import jax
import jax.numpy as jnp
import numpy as np
from jax import lax

LDEG = 72
ORDER = 10656
NT = 144
NP = 288
PANEL = 2048
ITERS = 2
N_COL = 8


def level_of(stream_key, dims, pieces, low, largest):
    loudness = 1.0
    for position, blocks in pieces:
        steps = jax.random.uniform(jax.random.fold_in(jax.random.fold_in(stream_key, 6), position), (blocks,), jnp.float32, low / len(pieces), largest / len(pieces))
        loudness = loudness * jnp.repeat(jnp.exp(steps), dims[position] // blocks).reshape((-1,) + (1,) * (len(dims) - 1 - position))
    return loudness


def noise(stream_key, dims, spread, most, pieces=(), kind=jnp.bfloat16):
    values = spread * jax.random.normal(stream_key, dims, jnp.float32)
    if pieces:
        values = values * level_of(stream_key, dims, pieces, -0.22, 0.18)
    return jnp.clip(values, -most, most).astype(kind)


def setup_inputs(seed: int = 0) -> dict:
    key_list = jax.random.split(jax.random.key(seed), 4)
    tmatrix = noise(key_list[0], (ORDER, ORDER), ORDER ** -0.5, 0.0625, ((0, 16), (1, 8)))
    panel = noise(key_list[1], (ORDER, PANEL), 1.0, 6.0, ((0, 8), (1, 16)))
    contrast = noise(key_list[2], (3, NT, NP), 0.3, 1.5, (), jnp.float32)
    return {"tmatrix": tmatrix, "panel": panel, "contrast": contrast}


def angular_tables(degree):
    lat_count = 2 * degree
    lon_count = 4 * degree
    freq_count = 2 * degree + 1
    colatitude = (np.arange(lat_count) + 0.5) * np.pi / lat_count
    cos_col = np.cos(colatitude)
    sin_col = np.sin(colatitude)
    legendre = np.zeros((freq_count, degree, lat_count))
    diagonal_term = np.full(lat_count, np.sqrt(0.5))
    for order_m in range(degree + 1):
        if order_m > 0:
            diagonal_term = diagonal_term * np.sqrt((2.0 * order_m + 1.0) / (2.0 * order_m)) * sin_col
        earlier = np.zeros(lat_count)
        latest = diagonal_term
        for degree_l in range(order_m, degree + 1):
            if degree_l == order_m:
                current = diagonal_term
            elif degree_l == order_m + 1:
                current = np.sqrt(2.0 * order_m + 3.0) * cos_col * diagonal_term
            else:
                factor_a = np.sqrt((4.0 * degree_l ** 2 - 1.0) / (degree_l ** 2 - order_m ** 2))
                factor_b = np.sqrt(((degree_l - 1.0) ** 2 - order_m ** 2) / (4.0 * (degree_l - 1.0) ** 2 - 1.0))
                current = factor_a * (cos_col * latest - factor_b * earlier)
            if degree_l > order_m:
                earlier, latest = (latest, current)
            if degree_l >= 1:
                legendre[order_m, degree_l - 1] = current
                if order_m >= 1:
                    legendre[degree + order_m, degree_l - 1] = current
    longitude = 2.0 * np.pi * np.arange(lon_count) / lon_count
    fourier = np.zeros((freq_count, lon_count))
    fourier[0] = 1.0 / np.sqrt(2.0 * np.pi)
    for order_m in range(1, degree + 1):
        fourier[order_m] = np.cos(order_m * longitude) / np.sqrt(np.pi)
        fourier[degree + order_m] = np.sin(order_m * longitude) / np.sqrt(np.pi)
    weight = sin_col * (np.pi / lat_count) * (2.0 * np.pi / lon_count)
    flat_list = []
    for freq_index in range(freq_count):
        order_m = freq_index if freq_index <= degree else freq_index - degree
        for level_index in range(degree):
            if level_index + 1 >= order_m:
                flat_list.append(freq_index * degree + level_index)
    flat_index = np.array(flat_list, dtype=np.int32)
    return (legendre, fourier, weight, flat_index)

def contrast_apply(coefficients, contrast, degree):
    legendre, fourier, weight, flat_index = angular_tables(degree)
    legendre = jnp.asarray(legendre, jnp.float32)
    fourier = jnp.asarray(fourier, jnp.float32)
    weight = jnp.asarray(weight, jnp.float32)
    freq_count, level_count = (legendre.shape[0], legendre.shape[1])
    columns = coefficients.shape[1]
    halves = coefficients.astype(jnp.float32).reshape(2, -1, columns)
    padded = jnp.zeros((2, freq_count * level_count, columns), jnp.float32).at[:, flat_index, :].set(halves)
    padded = padded.reshape(2, freq_count, level_count, columns)
    highest = lax.Precision.HIGHEST
    latitude = jnp.einsum('qlt,cqlk->cktq', legendre, padded, precision=highest)
    surface = jnp.einsum('cktq,qp->cktp', latitude, fourier, precision=highest)
    polar = contrast[0] * surface[0] + contrast[1] * surface[1]
    azimuth = contrast[1] * surface[0] + contrast[2] * surface[1]
    weighted = jnp.stack([polar, azimuth]) * weight[:, None]
    spectrum = jnp.einsum('cktp,qp->cktq', weighted, fourier, precision=highest)
    projected = jnp.einsum('qlt,cktq->cqlk', legendre, spectrum, precision=highest)
    picked = projected.reshape(2, freq_count * level_count, columns)[:, flat_index, :]
    return picked.reshape(-1, columns).astype(jnp.bfloat16)

def reference(tmatrix, panel, contrast):
    col_block = ORDER // N_COL
    map_width = min(128, PANEL)
    current = panel
    for iteration in range(ITERS):
        summed = jnp.zeros((ORDER, PANEL), jnp.float32)
        for block_index in range(N_COL):
            lower = block_index * col_block
            partial_value = jnp.dot(tmatrix[:, lower:lower + col_block], current[lower:lower + col_block], preferred_element_type=jnp.float32).astype(jnp.bfloat16)
            partial_value = lax.optimization_barrier(partial_value)
            summed = summed + partial_value.astype(jnp.float32)
        scattered = summed.astype(jnp.bfloat16)
        blocks = scattered.reshape(ORDER, PANEL // map_width, map_width).transpose(1, 0, 2)
        mapped = lax.map(lambda column_block: contrast_apply(column_block, contrast, LDEG), blocks)
        coupled = mapped.transpose(1, 0, 2).reshape(ORDER, PANEL)
        current = (panel.astype(jnp.float32) + coupled.astype(jnp.float32)).astype(jnp.bfloat16)
    return current
```

```python
import functools

import jax
import jax.numpy as jnp
import ml_dtypes
import numpy as np
from jax import lax
from jax.experimental import pallas as pl
from jax.experimental.pallas import tpu as pltpu
from jax.sharding import PartitionSpec as P

LDEG = 72
ITERS = 2
NT = 2 * LDEG
NP = 4 * LDEG
NQ = 2 * LDEG + 1
NX = 4
NZ = 4
NY = 4
ROWS = 16
COLS = 8
BLK = 666
HALF = 672
QUART = HALF // 2
LANES = 768
WIN = LANES // 128
TPAD = 256
QPAD = 160
PER = 16
MIB = 1024 * 1024
MESH = pl.DeviceIdType.MESH


def angular_tables(degree):
    lat_count = 2 * degree
    lon_count = 4 * degree
    freq_count = 2 * degree + 1
    colatitude = (np.arange(lat_count) + 0.5) * np.pi / lat_count
    cos_col = np.cos(colatitude)
    sin_col = np.sin(colatitude)
    legendre = np.zeros((freq_count, degree, lat_count))
    diagonal_term = np.full(lat_count, np.sqrt(0.5))
    for order_m in range(degree + 1):
        if order_m > 0:
            diagonal_term = (
                diagonal_term * np.sqrt((2.0 * order_m + 1.0) / (2.0 * order_m)) * sin_col
            )
        earlier = np.zeros(lat_count)
        latest = diagonal_term
        for degree_l in range(order_m, degree + 1):
            if degree_l == order_m:
                current = diagonal_term
            elif degree_l == order_m + 1:
                current = np.sqrt(2.0 * order_m + 3.0) * cos_col * diagonal_term
            else:
                factor_a = np.sqrt((4.0 * degree_l**2 - 1.0) / (degree_l**2 - order_m**2))
                factor_b = np.sqrt(
                    ((degree_l - 1.0) ** 2 - order_m**2) / (4.0 * (degree_l - 1.0) ** 2 - 1.0)
                )
                current = factor_a * (cos_col * latest - factor_b * earlier)
            if degree_l > order_m:
                earlier, latest = (latest, current)
            if degree_l >= 1:
                legendre[order_m, degree_l - 1] = current
                if order_m >= 1:
                    legendre[degree + order_m, degree_l - 1] = current
    longitude = 2.0 * np.pi * np.arange(lon_count) / lon_count
    fourier = np.zeros((freq_count, lon_count))
    fourier[0] = 1.0 / np.sqrt(2.0 * np.pi)
    for order_m in range(1, degree + 1):
        fourier[order_m] = np.cos(order_m * longitude) / np.sqrt(np.pi)
        fourier[degree + order_m] = np.sin(order_m * longitude) / np.sqrt(np.pi)
    weight = sin_col * (np.pi / lat_count) * (2.0 * np.pi / lon_count)
    return (legendre, fourier, weight)


def meetings():
    owner = []
    for q in range(NQ):
        m = q if q <= LDEG else q - LDEG
        owner += [(q, l) for l in range(max(m, 1), LDEG + 1)]
    found = []
    for block in range(ROWS // 2):
        for window in range(WIN):
            first = block * BLK + window * 128
            last = min(first + 128, (block + 1) * BLK)
            for q in sorted({owner[n][0] for n in range(first, last)}):
                rows = [(n - first, owner[n][1] - 1) for n in range(first, last) if owner[n][0] == q]
                found.append((block, window, q, rows))
    return found


def split(table):
    high = table.astype(np.float32).astype(ml_dtypes.bfloat16)
    low = (table - high.astype(np.float64)).astype(np.float32).astype(ml_dtypes.bfloat16)
    return np.stack([high, low])


@functools.lru_cache(None)
def tables():
    legendre, fourier, weight = angular_tables(LDEG)
    found = meetings()
    windows = np.zeros((len(found), 128, TPAD))
    for index, (block, window, q, rows) in enumerate(found):
        for place, level in rows:
            windows[index, place, :NT] = legendre[q, level]
    padded = np.zeros((QPAD, NP))
    padded[:NQ] = fourier
    return (
        [f[:3] for f in found],
        windows.astype(np.float32).astype(ml_dtypes.bfloat16),
        split(np.ascontiguousarray(padded.T)),
        split(padded),
        weight.astype(np.float32),
    )


def dot(a, b):
    return jnp.dot(a, b, preferred_element_type=jnp.float32)


def two(value):
    high = value.astype(jnp.bfloat16)
    return high, (value - high.astype(jnp.float32)).astype(jnp.bfloat16)


def coupling_kernel(found, s_ref, w_ref, fs_ref, fa_ref, cw_ref, b_ref, lat, spec):
    by_q = {}
    by_window = {}
    for index, (block, window, q) in enumerate(found):
        by_q.setdefault(q, []).append((index, block, window))
        by_window.setdefault((block, window), []).append((index, q))

    def coefficients(block, window):
        lanes = slice(window * 128, (window + 1) * 128)
        return jnp.concatenate([s_ref[block, :, lanes], s_ref[block + 8, :, lanes]], axis=0)

    for q in range(NQ):
        total = None
        for index, block, window in by_q[q]:
            term = dot(coefficients(block, window), w_ref[index])
            total = term if total is None else total + term
        for half in range(2):
            lat[half, q * 32 : (q + 1) * 32, :] = total[:, half * 128 : half * 128 + 128]
    lat[:, NQ * 32 :, :] = jnp.zeros((2, QPAD * 32 - NQ * 32, 128), jnp.float32)

    def synthesis(place):
        rows = pl.ds(place, QPAD, stride=32)
        high, low = two(jnp.concatenate([lat[0, rows, :], lat[1, rows, :]], axis=1))
        return dot(fs_ref[0], high) + dot(fs_ref[1], high) + dot(fs_ref[0], low)

    def analysis(place, value):
        high, low = two(value)
        value = dot(fa_ref[0], high) + dot(fa_ref[1], high) + dot(fa_ref[0], low)
        for half in range(2):
            spec[half, pl.ds(place, QPAD, stride=32), :] = value[:, half * 128 : half * 128 + 128]

    def column(k, carry):
        first = synthesis(k)
        second = synthesis(PER + k)
        analysis(k, cw_ref[0] * first + cw_ref[1] * second)
        analysis(PER + k, cw_ref[1] * first + cw_ref[2] * second)
        return carry

    lax.fori_loop(0, PER, column, 0)

    for (block, window), members in sorted(by_window.items()):
        total = None
        for index, q in members:
            rows = slice(q * 32, (q + 1) * 32)
            high, low = two(jnp.concatenate([spec[0, rows, :], spec[1, rows, :]], axis=1))
            term = lax.dot_general(
                jnp.concatenate([high, low], axis=0),
                w_ref[index],
                (((1,), (1,)), ((), ())),
                preferred_element_type=jnp.float32,
            )
            total = term if total is None else total + term
        value = (total[:32] + total[32:]).astype(jnp.bfloat16)
        lanes = slice(window * 128, (window + 1) * 128)
        b_ref[block, :, lanes] = value[:PER]
        b_ref[block + 8, :, lanes] = value[PER:]


def coupling(s, w, fs, fa, cw, found):
    vmem = pl.BlockSpec(memory_space=pltpu.VMEM)
    return pl.pallas_call(
        functools.partial(coupling_kernel, found),
        out_shape=jax.ShapeDtypeStruct((ROWS, PER, LANES), jnp.bfloat16),
        in_specs=[vmem] * 5,
        out_specs=vmem,
        scratch_shapes=[
            pltpu.VMEM((2, QPAD * 32, 128), jnp.float32),
            pltpu.VMEM((2, QPAD * 32, 128), jnp.float32),
        ],
        compiler_params=pltpu.CompilerParams(vmem_limit_bytes=48 * MIB),
        name="coupling",
    )(s, w, fs, fa, cw)


STEP = {"x+": (1, 0), "x-": (-1, 0), "z+": (0, 1), "z-": (0, -1)}
ALL = (0, 2 * HALF)
A = (0, HALF)
B = (HALF, HALF)
A0, A1 = (0, QUART), (QUART, QUART)
B0, B1 = (HALF, QUART), (HALF + QUART, QUART)


def ring_plan():
    plan = []

    def send(part, rel, way):
        plan.append(("send", part, (rel[0] % NX, rel[1] % NZ), way))

    def recv(part, rel, way):
        plan.append(("recv", part, (rel[0] % NX, rel[1] % NZ), way))

    def use(*rels):
        for rel in rels:
            plan.append(("use", (rel[0] % NX, rel[1] % NZ)))

    own = (0, 0)
    for way in ("x+", "x-"):
        send(A, own, way)
    for way in ("z+", "z-"):
        send(B, own, way)
    for way in ("z+", "z-"):
        send(A, own, way)
    for way in ("x+", "x-"):
        send(B, own, way)
    use(own)
    for part, quart, rel, way in ((A, A0, (-1, 0), "x+"), (A, A1, (1, 0), "x-")):
        recv(part, rel, way)
        send(quart, rel, way)
        send(A, rel, "z+")
        send(A, rel, "z-")
    for part, quart, rel, way in ((B, B0, (0, -1), "z+"), (B, B1, (0, 1), "z-")):
        recv(part, rel, way)
        send(quart, rel, way)
        send(B, rel, "x+")
        send(B, rel, "x-")
    for quart, rel, way in ((A0, (0, -1), "z+"), (A1, (0, 1), "z-")):
        recv(A, rel, way)
        send(quart, rel, way)
    for quart, rel, way in ((B0, (-1, 0), "x+"), (B1, (1, 0), "x-")):
        recv(B, rel, way)
        send(quart, rel, way)
    use((-1, 0), (1, 0))
    recv(A0, (2, 0), "x+")
    recv(A1, (2, 0), "x-")
    send(A, (2, 0), "z+")
    send(A, (2, 0), "z-")
    recv(B0, (0, 2), "z+")
    recv(B1, (0, 2), "z-")
    send(B, (0, 2), "x+")
    send(B, (0, 2), "x-")
    use((0, -1), (0, 1))
    for x in (-1, 1):
        for quart, z, way in ((A0, -1, "z+"), (A1, 1, "z-")):
            recv(A, (x, z), way)
            send(quart, (x, z), way)
    for z in (-1, 1):
        for quart, x, way in ((B0, -1, "x+"), (B1, 1, "x-")):
            recv(B, (x, z), way)
            send(quart, (x, z), way)
    use((-1, -1), (-1, 1))
    recv(A0, (0, 2), "z+")
    recv(A1, (0, 2), "z-")
    recv(B0, (2, 0), "x+")
    recv(B1, (2, 0), "x-")
    for quart, z, way in ((A0, -1, "z+"), (A1, 1, "z-")):
        recv(A, (2, z), way)
        send(quart, (2, z), way)
    for quart, x, way in ((B0, -1, "x+"), (B1, 1, "x-")):
        recv(B, (x, 2), way)
        send(quart, (x, 2), way)
    use((1, -1), (1, 1), (0, 2), (2, 0))
    for x in (-1, 1):
        recv(A0, (x, 2), "z+")
        recv(A1, (x, 2), "z-")
        use((x, 2))
    for z in (-1, 1):
        recv(B0, (2, z), "x+")
        recv(B1, (2, z), "x-")
        use((2, z))
    recv(A0, (2, 2), "z+")
    recv(A1, (2, 2), "z-")
    recv(B0, (2, 2), "x+")
    recv(B1, (2, 2), "x-")
    use((2, 2))
    return plan


def greet(others):
    barrier = pltpu.get_barrier_semaphore()
    for other in others:
        pl.semaphore_signal(barrier, inc=1, device_id=other, device_id_type=MESH)
    pl.semaphore_wait(barrier, len(others))


def product_kernel(
    plan,
    t_ref,
    u_ref,
    s_ref,
    held,
    prod,
    mate_out,
    mate_in,
    sums,
    y_in,
    z_out,
    own_sem,
    ring_send,
    ring_recv,
    mate_send,
    mate_recv,
    y_send,
    y_recv,
    z_send,
    z_recv,
    last_sem,
):
    row = lax.axis_index("row")
    col = lax.axis_index("col")
    x, z = row // NZ, row % NZ
    y, core = col // 2, col % 2

    def block_of(rel):
        return ((x + rel[0] + NX) % NX) * NZ + (z + rel[1] + NZ) % NZ

    own_copy = pltpu.make_async_copy(u_ref, held.at[row], own_sem)
    own_copy.start()
    row_peers = [{"row": (row + k) % ROWS} for k in range(1, ROWS)]
    mate = {"col": y * 2 + (1 - core)}
    y_peers = [{"col": ((y + k) % NY) * 2 + core} for k in range(1, NY)]
    greet(row_peers + [mate] + y_peers)

    slot = {}
    for event in plan:
        if event[0] == "send":
            slot[event[1:]] = len(slot)

    def ring_copy(part, rel, way, number, source=None):
        target = block_of(STEP[way])
        block = block_of(rel)
        rows = pl.ds(part[0], part[1])
        here = held.at[block, rows]
        return pltpu.make_async_remote_copy(
            src_ref=here if source is None else source.at[rows],
            dst_ref=here,
            send_sem=ring_send.at[number],
            recv_sem=ring_recv.at[number],
            device_id={"row": target},
            device_id_type=MESH,
        )

    def mate_copy(s):
        return pltpu.make_async_remote_copy(
            src_ref=mate_out.at[s],
            dst_ref=mate_in.at[s],
            send_sem=mate_send.at[s],
            recv_sem=mate_recv.at[s],
            device_id=mate,
            device_id_type=MESH,
        )

    def y_copy(s, k):
        to = (y + k) % NY
        number = s * 3 + k - 1
        return pltpu.make_async_remote_copy(
            src_ref=sums.at[s, pl.ds(pl.multiple_of(to * PER, PER), PER)],
            dst_ref=y_in.at[s, k - 1],
            send_sem=y_send.at[number],
            recv_sem=y_recv.at[number],
            device_id=y_peers[k - 1],
            device_id_type=MESH,
        )

    order = [event[1] for event in plan if event[0] == "use"]

    def z_copy(s):
        return pltpu.make_async_remote_copy(
            src_ref=z_out.at[s],
            dst_ref=s_ref.at[row],
            send_sem=z_send.at[s],
            recv_sem=z_recv.at[s],
            device_id={"row": block_of(order[s])},
            device_id_type=MESH,
        )

    def z_arrival(s):
        back = (-order[s][0], -order[s][1])
        return pltpu.make_async_remote_copy(
            src_ref=z_out.at[s],
            dst_ref=s_ref.at[block_of(back)],
            send_sem=z_send.at[s],
            recv_sem=z_recv.at[s],
            device_id={"row": block_of(back)},
            device_id_type=MESH,
        )

    def multiply(s, rel):
        block = block_of(rel)
        here = s % 2
        for chunk in range(LANES // 256):
            rows = slice(chunk * 256, (chunk + 1) * 256)
            value = dot(t_ref[0, rows], held[block, 0:HALF]) + dot(t_ref[1, rows], held[block, HALF : 2 * HALF])
            prod[here, :, rows] = value.T
        start = pl.multiple_of((1 - core) * 64, 64)
        mate_out[s] = prod[here, pl.ds(start, 64), :].astype(jnp.bfloat16)
        mate_copy(s).start()

    def add_mate(s):
        mate_copy(s).wait_recv()
        start = pl.multiple_of(core * 64, 64)
        sums[s] = (prod[s % 2, pl.ds(start, 64), :] + mate_in[s].astype(jnp.float32)).astype(jnp.bfloat16)
        for k in (2, 1, 3):
            y_copy(s, k).start()

    def add_y(s):
        total = sums[s, pl.ds(pl.multiple_of(y * PER, PER), PER)].astype(jnp.float32)
        for k in range(1, NY):
            y_copy(s, k).wait_recv()
            total += y_in[s, k - 1].astype(jnp.float32)
        z_out[s] = total.astype(jnp.bfloat16)
        if s == 0:
            pltpu.make_async_copy(z_out.at[0], s_ref.at[row], last_sem).start()
        else:
            z_copy(s).start()

    s = 0
    first = True
    for event in plan:
        if event[0] == "send":
            _, part, rel, way = event
            ring_copy(part, rel, way, slot[event[1:]], u_ref if rel == (0, 0) else None).start()
        elif event[0] == "recv":
            _, part, rel, way = event
            there = ((rel[0] + STEP[way][0]) % NX, (rel[1] + STEP[way][1]) % NZ)
            ring_copy(part, rel, way, slot[(part, there, way)]).wait_recv()
        else:
            if first:
                own_copy.wait()
                first = False
            multiply(s, event[1])
            if s >= 1:
                add_mate(s - 1)
            if s >= 3:
                add_y(s - 3)
            s += 1
    add_mate(ROWS - 1)
    for s in (ROWS - 3, ROWS - 2, ROWS - 1):
        add_y(s)
    for event in plan:
        if event[0] == "send":
            _, part, rel, way = event
            ring_copy(part, rel, way, slot[event[1:]], u_ref if rel == (0, 0) else None).wait_send()
    for s in range(ROWS):
        mate_copy(s).wait_send()
        for k in range(1, NY):
            y_copy(s, k).wait_send()
    pltpu.make_async_copy(z_out.at[0], s_ref.at[row], last_sem).wait()
    for s in range(1, ROWS):
        z_arrival(s).wait_recv()
        z_copy(s).wait_send()


def product(t, u):
    plan = ring_plan()
    sends = sum(event[0] == "send" for event in plan)
    vmem = pl.BlockSpec(memory_space=pltpu.VMEM)
    dma = pltpu.SemaphoreType.DMA
    bf16 = jnp.bfloat16
    return pl.pallas_call(
        functools.partial(product_kernel, plan),
        out_shape=jax.ShapeDtypeStruct((ROWS, PER, LANES), bf16),
        in_specs=[vmem] * 2,
        out_specs=vmem,
        scratch_shapes=[
            pltpu.VMEM((ROWS, 2 * HALF, 128), bf16),
            pltpu.VMEM((2, 128, LANES), jnp.float32),
            pltpu.VMEM((ROWS, 64, LANES), bf16),
            pltpu.VMEM((ROWS, 64, LANES), bf16),
            pltpu.VMEM((ROWS, 64, LANES), bf16),
            pltpu.VMEM((ROWS, NY - 1, PER, LANES), bf16),
            pltpu.VMEM((ROWS, PER, LANES), bf16),
            dma(()),
            dma((sends,)),
            dma((sends,)),
            dma((ROWS,)),
            dma((ROWS,)),
            dma((ROWS * 3,)),
            dma((ROWS * 3,)),
            dma((ROWS,)),
            dma((ROWS,)),
            dma(()),
        ],
        compiler_params=pltpu.CompilerParams(
            collective_id=0, has_side_effects=True, vmem_limit_bytes=40 * MIB
        ),
        name="product",
    )(t, u)


def return_kernel(b_ref, panel_ref, u_ref, came, send_sem, recv_sem, own_sem):
    col = lax.axis_index("col")
    y, core = col // 2, col % 2
    peers = []
    for dy in range(NY):
        for dc in range(2):
            peers.append((((y + dy) % NY), (core + dc) % 2))
    greet([{"col": py * 2 + pc} for py, pc in peers[1:]])
    mine = core * NY + y

    def copy(k):
        py, pc = peers[k]
        return pltpu.make_async_remote_copy(
            src_ref=b_ref.at[pl.ds((py * 2 + pc) * 2, 2)],
            dst_ref=came.at[mine],
            send_sem=send_sem.at[k],
            recv_sem=recv_sem.at[k],
            device_id={"col": py * 2 + pc},
            device_id_type=MESH,
        )

    def arrival(k):
        dy, dc = k // 2, k % 2
        py, pc = (y - dy + NY) % NY, (core + dc) % 2
        return pltpu.make_async_remote_copy(
            src_ref=b_ref.at[pl.ds(0, 2)],
            dst_ref=came.at[pc * NY + py],
            send_sem=send_sem.at[k],
            recv_sem=recv_sem.at[k],
            device_id={"col": py * 2 + pc},
            device_id_type=MESH,
        )

    for k in range(1, COLS):
        copy(k).start()
    own = pltpu.make_async_copy(b_ref.at[pl.ds(col * 2, 2)], came.at[mine], own_sem)
    own.start()
    own.wait()
    for k in range(1, COLS):
        arrival(k).wait_recv()
    for half in range(2):
        value = jnp.concatenate([came[k, half].astype(jnp.float32) for k in range(COLS)], axis=0)
        value = value.T[:HALF] + panel_ref[half].astype(jnp.float32)
        u_ref[half * HALF : (half + 1) * HALF, :] = value.astype(jnp.bfloat16)
    for k in range(1, COLS):
        copy(k).wait_send()


def give_back(b, panel):
    vmem = pl.BlockSpec(memory_space=pltpu.VMEM)
    dma = pltpu.SemaphoreType.DMA
    return pl.pallas_call(
        return_kernel,
        out_shape=jax.ShapeDtypeStruct((2 * HALF, 128), jnp.bfloat16),
        in_specs=[vmem] * 2,
        out_specs=vmem,
        scratch_shapes=[
            pltpu.VMEM((COLS, 2, PER, LANES), jnp.bfloat16),
            dma((COLS,)),
            dma((COLS,)),
            dma(()),
        ],
        compiler_params=pltpu.CompilerParams(
            collective_id=1, has_side_effects=True, vmem_limit_bytes=16 * MIB
        ),
        name="give_back",
    )(b, panel)


def body(tmatrix, panel, contrast):
    found, windows, fs, fa, weight = tables()
    w = jnp.asarray(windows)
    fs = jnp.asarray(fs)
    fa = jnp.asarray(fa)
    cw = jnp.transpose(contrast * jnp.asarray(weight)[None, :, None], (0, 2, 1))
    cw = jnp.pad(cw, ((0, 0), (0, 0), (0, TPAD - NT)))
    t = jnp.stack([tmatrix[:, :BLK], tmatrix[:, BLK:]])
    t = jnp.pad(t, ((0, 0), (0, LANES - BLK), (0, HALF - BLK)))
    pad = jnp.pad(panel.reshape(2, BLK, 128), ((0, 0), (0, HALF - BLK), (0, 0)))
    u = pad.reshape(2 * HALF, 128)
    for iteration in range(ITERS):
        s = product(t, u)
        b = coupling(s, w, fs, fa, cw, found)
        u = give_back(b, pad)
    return jnp.concatenate([u[:BLK], u[HALF : HALF + BLK]], axis=0)


def solution(mesh):
    placed = (P("row", "col"), P("col", "row"), P())
    return jax.shard_map(
        body, mesh=mesh, in_specs=placed, out_specs=P("col", "row"), check_vma=False
    )
```

```python
import functools

import jax
import jax.numpy as jnp
import ml_dtypes
import numpy as np
from jax import lax
from jax.experimental import pallas as pl
from jax.experimental.pallas import tpu as pltpu
from jax.sharding import PartitionSpec as P

LDEG = 72
ITERS = 2
NT = 2 * LDEG
NP = 4 * LDEG
NQ = 2 * LDEG + 1
NX = 4
NZ = 4
NY = 4
ROWS = 16
COLS = 8
BLK = 666
HALF = 672
QUART = HALF // 2
LANES = 768
WIN = LANES // 128
TPAD = 256
QPAD = 160
PER = 16
MIB = 1024 * 1024
MESH = pl.DeviceIdType.MESH


def angular_tables(degree):
    lat_count = 2 * degree
    lon_count = 4 * degree
    freq_count = 2 * degree + 1
    colatitude = (np.arange(lat_count) + 0.5) * np.pi / lat_count
    cos_col = np.cos(colatitude)
    sin_col = np.sin(colatitude)
    legendre = np.zeros((freq_count, degree, lat_count))
    diagonal_term = np.full(lat_count, np.sqrt(0.5))
    for order_m in range(degree + 1):
        if order_m > 0:
            diagonal_term = (
                diagonal_term * np.sqrt((2.0 * order_m + 1.0) / (2.0 * order_m)) * sin_col
            )
        earlier = np.zeros(lat_count)
        latest = diagonal_term
        for degree_l in range(order_m, degree + 1):
            if degree_l == order_m:
                current = diagonal_term
            elif degree_l == order_m + 1:
                current = np.sqrt(2.0 * order_m + 3.0) * cos_col * diagonal_term
            else:
                factor_a = np.sqrt((4.0 * degree_l**2 - 1.0) / (degree_l**2 - order_m**2))
                factor_b = np.sqrt(
                    ((degree_l - 1.0) ** 2 - order_m**2) / (4.0 * (degree_l - 1.0) ** 2 - 1.0)
                )
                current = factor_a * (cos_col * latest - factor_b * earlier)
            if degree_l > order_m:
                earlier, latest = (latest, current)
            if degree_l >= 1:
                legendre[order_m, degree_l - 1] = current
                if order_m >= 1:
                    legendre[degree + order_m, degree_l - 1] = current
    longitude = 2.0 * np.pi * np.arange(lon_count) / lon_count
    fourier = np.zeros((freq_count, lon_count))
    fourier[0] = 1.0 / np.sqrt(2.0 * np.pi)
    for order_m in range(1, degree + 1):
        fourier[order_m] = np.cos(order_m * longitude) / np.sqrt(np.pi)
        fourier[degree + order_m] = np.sin(order_m * longitude) / np.sqrt(np.pi)
    weight = sin_col * (np.pi / lat_count) * (2.0 * np.pi / lon_count)
    return (legendre, fourier, weight)


def meetings():
    owner = []
    for q in range(NQ):
        m = q if q <= LDEG else q - LDEG
        owner += [(q, l) for l in range(max(m, 1), LDEG + 1)]
    found = []
    for block in range(ROWS // 2):
        for window in range(WIN):
            first = block * BLK + window * 128
            last = min(first + 128, (block + 1) * BLK)
            for q in sorted({owner[n][0] for n in range(first, last)}):
                rows = [(n - first, owner[n][1] - 1) for n in range(first, last) if owner[n][0] == q]
                found.append((block, window, q, rows))
    return found


def split(table):
    high = table.astype(np.float32).astype(ml_dtypes.bfloat16)
    low = (table - high.astype(np.float64)).astype(np.float32).astype(ml_dtypes.bfloat16)
    return np.stack([high, low])


@functools.lru_cache(None)
def tables():
    legendre, fourier, weight = angular_tables(LDEG)
    found = meetings()
    windows = np.zeros((len(found), 128, TPAD))
    for index, (block, window, q, rows) in enumerate(found):
        for place, level in rows:
            windows[index, place, :NT] = legendre[q, level]
    padded = np.zeros((QPAD, NP))
    padded[:NQ] = fourier
    return (
        [f[:3] for f in found],
        windows.astype(np.float32).astype(ml_dtypes.bfloat16),
        split(np.ascontiguousarray(padded.T)),
        split(padded),
        weight.astype(np.float32),
    )


def dot(a, b):
    return jnp.dot(a, b, preferred_element_type=jnp.float32)


def two(value):
    high = value.astype(jnp.bfloat16)
    return high, (value - high.astype(jnp.float32)).astype(jnp.bfloat16)


def legendre_in(found, coefficients, w_ref, lat):
    by_q = {}
    for index, (block, window, q) in enumerate(found):
        by_q.setdefault(q, []).append((index, block, window))
    for q in range(NQ):
        total = None
        for index, block, window in by_q[q]:
            term = dot(coefficients(block, window), w_ref[index])
            total = term if total is None else total + term
        for half in range(2):
            lat[half, q * 32 : (q + 1) * 32, :] = total[:, half * 128 : half * 128 + 128]


def columns(fs_ref, fa_ref, cw_ref, lat, spec):
    def synthesis(place):
        rows = pl.ds(place, QPAD, stride=32)
        high, low = two(jnp.concatenate([lat[0, rows, :], lat[1, rows, :]], axis=1))
        return dot(fs_ref[0], high) + dot(fs_ref[1], high) + dot(fs_ref[0], low)

    def analysis(place, value):
        high, low = two(value)
        value = dot(fa_ref[0], high) + dot(fa_ref[1], high) + dot(fa_ref[0], low)
        for half in range(2):
            spec[half, pl.ds(place, QPAD, stride=32), :] = value[:, half * 128 : half * 128 + 128]

    def column(k, carry):
        first = synthesis(k)
        second = synthesis(PER + k)
        analysis(k, cw_ref[0] * first + cw_ref[1] * second)
        analysis(PER + k, cw_ref[1] * first + cw_ref[2] * second)
        return carry

    lax.fori_loop(0, PER, column, 0, unroll=2)


def legendre_out(found, w_ref, spec, b_ref, done):
    by_window = {}
    for index, (block, window, q) in enumerate(found):
        by_window.setdefault((block, window), []).append((index, q))
    for (block, window), members in sorted(by_window.items()):
        total = None
        for index, q in members:
            rows = slice(q * 32, (q + 1) * 32)
            high, low = two(jnp.concatenate([spec[0, rows, :], spec[1, rows, :]], axis=1))
            term = lax.dot_general(
                jnp.concatenate([high, low], axis=0),
                w_ref[index],
                (((1,), (1,)), ((), ())),
                preferred_element_type=jnp.float32,
            )
            total = term if total is None else total + term
        value = (total[:32] + total[32:]).astype(jnp.bfloat16)
        lanes = slice(window * 128, (window + 1) * 128)
        b_ref[block, :, lanes] = value[:PER]
        b_ref[block + 8, :, lanes] = value[PER:]
        if window == WIN - 1 and block % 2 == 1:
            done(block // 2)
            done(block // 2 + 4)


STEP = {"x+": (1, 0), "x-": (-1, 0), "z+": (0, 1), "z-": (0, -1)}
ALL = (0, 2 * HALF)
A = (0, HALF)
B = (HALF, HALF)
A0, A1 = (0, QUART), (QUART, QUART)
B0, B1 = (HALF, QUART), (HALF + QUART, QUART)


def ring_plan():
    plan = []

    def send(part, rel, way):
        plan.append(("send", part, (rel[0] % NX, rel[1] % NZ), way))

    def recv(part, rel, way):
        plan.append(("recv", part, (rel[0] % NX, rel[1] % NZ), way))

    def use(*rels):
        for rel in rels:
            plan.append(("use", (rel[0] % NX, rel[1] % NZ)))

    own = (0, 0)
    for way in ("x+", "x-"):
        send(A, own, way)
    for way in ("z+", "z-"):
        send(B, own, way)
    for way in ("z+", "z-"):
        send(A, own, way)
    for way in ("x+", "x-"):
        send(B, own, way)
    use(own)
    for part, quart, rel, way in ((A, A0, (-1, 0), "x+"), (A, A1, (1, 0), "x-")):
        recv(part, rel, way)
        send(quart, rel, way)
        send(A, rel, "z+")
        send(A, rel, "z-")
    for part, quart, rel, way in ((B, B0, (0, -1), "z+"), (B, B1, (0, 1), "z-")):
        recv(part, rel, way)
        send(quart, rel, way)
        send(B, rel, "x+")
        send(B, rel, "x-")
    for quart, rel, way in ((A0, (0, -1), "z+"), (A1, (0, 1), "z-")):
        recv(A, rel, way)
        send(quart, rel, way)
    for quart, rel, way in ((B0, (-1, 0), "x+"), (B1, (1, 0), "x-")):
        recv(B, rel, way)
        send(quart, rel, way)
    use((-1, 0), (1, 0))
    recv(A0, (2, 0), "x+")
    recv(A1, (2, 0), "x-")
    send(A, (2, 0), "z+")
    send(A, (2, 0), "z-")
    recv(B0, (0, 2), "z+")
    recv(B1, (0, 2), "z-")
    send(B, (0, 2), "x+")
    send(B, (0, 2), "x-")
    use((0, -1), (0, 1))
    for x in (-1, 1):
        for quart, z, way in ((A0, -1, "z+"), (A1, 1, "z-")):
            recv(A, (x, z), way)
            send(quart, (x, z), way)
    for z in (-1, 1):
        for quart, x, way in ((B0, -1, "x+"), (B1, 1, "x-")):
            recv(B, (x, z), way)
            send(quart, (x, z), way)
    use((-1, -1), (-1, 1))
    recv(A0, (0, 2), "z+")
    recv(A1, (0, 2), "z-")
    recv(B0, (2, 0), "x+")
    recv(B1, (2, 0), "x-")
    for quart, z, way in ((A0, -1, "z+"), (A1, 1, "z-")):
        recv(A, (2, z), way)
        send(quart, (2, z), way)
    for quart, x, way in ((B0, -1, "x+"), (B1, 1, "x-")):
        recv(B, (x, 2), way)
        send(quart, (x, 2), way)
    use((1, -1), (1, 1), (0, 2), (2, 0))
    for x in (-1, 1):
        recv(A0, (x, 2), "z+")
        recv(A1, (x, 2), "z-")
        use((x, 2))
    for z in (-1, 1):
        recv(B0, (2, z), "x+")
        recv(B1, (2, z), "x-")
        use((2, z))
    recv(A0, (2, 2), "z+")
    recv(A1, (2, 2), "z-")
    recv(B0, (2, 2), "x+")
    recv(B1, (2, 2), "x-")
    use((2, 2))
    return plan


def greet(others):
    barrier = pltpu.get_barrier_semaphore()
    for other in others:
        pl.semaphore_signal(barrier, inc=1, device_id=other, device_id_type=MESH)
    pl.semaphore_wait(barrier, len(others))


def step_kernel(
    plan,
    found,
    t_ref,
    panel_ref,
    contrast_ref,
    weight_ref,
    w_hbm,
    fs_ref,
    fa_ref,
    out_ref,
    held,
    prod,
    mate_out,
    mate_in,
    sums,
    y_in,
    z_out,
    s_in,
    b_out,
    b_in,
    w_ref,
    cw_ref,
    lat,
    spec,
    w_sem,
    ring_send,
    ring_recv,
    mate_send,
    mate_recv,
    y_send,
    y_recv,
    z_send,
    z_recv,
    b_send,
    b_recv,
):
    row = lax.axis_index("row")
    col = lax.axis_index("col")
    x, z = row // NZ, row % NZ
    y, core = col // 2, col % 2
    f32, bf16 = jnp.float32, jnp.bfloat16

    def block_of(rel):
        return ((x + rel[0] + NX) % NX) * NZ + (z + rel[1] + NZ) % NZ

    table_copy = pltpu.make_async_copy(w_hbm, w_ref, w_sem)
    table_copy.start()
    held[0, row] = panel_ref[...]
    greet(
        [{"row": (row + k) % ROWS} for k in range(1, ROWS)]
        + [{"col": (col + k) % COLS} for k in range(1, COLS)]
    )
    mate = {"col": y * 2 + (1 - core)}
    y_peers = [{"col": ((y + k) % NY) * 2 + core} for k in range(1, NY)]

    slot = {}
    for event in plan:
        if event[0] == "send":
            slot[event[1:]] = len(slot)
    order = [event[1] for event in plan if event[0] == "use"]

    def ring_copy(it, part, rel, way, number):
        here = held.at[it, block_of(rel), pl.ds(part[0], part[1])]
        return pltpu.make_async_remote_copy(
            src_ref=here,
            dst_ref=here,
            send_sem=ring_send.at[number],
            recv_sem=ring_recv.at[it, number],
            device_id={"row": block_of(STEP[way])},
            device_id_type=MESH,
        )

    def mate_copy(it, s):
        return pltpu.make_async_remote_copy(
            src_ref=mate_out.at[s],
            dst_ref=mate_in.at[it, s],
            send_sem=mate_send.at[s],
            recv_sem=mate_recv.at[it, s],
            device_id=mate,
            device_id_type=MESH,
        )

    def y_copy(it, s, k):
        to = (y + k) % NY
        number = s * 3 + k - 1
        return pltpu.make_async_remote_copy(
            src_ref=sums.at[s, pl.ds(pl.multiple_of(to * PER, PER), PER)],
            dst_ref=y_in.at[it, s, k - 1],
            send_sem=y_send.at[number],
            recv_sem=y_recv.at[it, number],
            device_id=y_peers[k - 1],
            device_id_type=MESH,
        )

    def z_copy(it, s):
        return pltpu.make_async_remote_copy(
            src_ref=z_out.at[s],
            dst_ref=s_in.at[it, row],
            send_sem=z_send.at[s],
            recv_sem=z_recv.at[it, s],
            device_id={"row": block_of(order[s])},
            device_id_type=MESH,
        )

    def z_arrival(it, s):
        back = (-order[s][0], -order[s][1])
        return pltpu.make_async_remote_copy(
            src_ref=z_out.at[s],
            dst_ref=s_in.at[it, block_of(back)],
            send_sem=z_send.at[s],
            recv_sem=z_recv.at[it, s],
            device_id={"row": block_of(back)},
            device_id_type=MESH,
        )

    def b_copy(it, k):
        return pltpu.make_async_remote_copy(
            src_ref=b_out.at[pl.ds(2 * k, 2)],
            dst_ref=b_in.at[it, core * NY + y],
            send_sem=b_send.at[k],
            recv_sem=b_recv.at[it, col],
            device_id={"col": k},
            device_id_type=MESH,
        )

    def b_arrival(it, k):
        return pltpu.make_async_remote_copy(
            src_ref=b_out.at[pl.ds(2 * k, 2)],
            dst_ref=b_in.at[it, k % 2 * NY + k // 2],
            send_sem=b_send.at[k],
            recv_sem=b_recv.at[it, k],
            device_id={"col": k},
            device_id_type=MESH,
        )

    def multiply(it, s, rel):
        block = block_of(rel)
        here = s % 4
        for chunk in range(LANES // 256):
            rows = slice(chunk * 256, (chunk + 1) * 256)
            value = dot(t_ref[0, rows], held[it, block, 0:HALF])
            value += dot(t_ref[1, rows], held[it, block, HALF : 2 * HALF])
            prod[here, :, rows] = value.T
        start = pl.multiple_of((1 - core) * 64, 64)
        mate_out[s] = prod[here, pl.ds(start, 64), :].astype(bf16)
        mate_copy(it, s).start()

    def add_mate(it, s):
        mate_copy(it, s).wait_recv()
        start = pl.multiple_of(core * 64, 64)
        sums[s] = (prod[s % 4, pl.ds(start, 64), :] + mate_in[it, s].astype(f32)).astype(bf16)
        for k in (2, 1, 3):
            y_copy(it, s, k).start()

    def add_y(it, s):
        total = sums[s, pl.ds(pl.multiple_of(y * PER, PER), PER)].astype(f32)
        for k in range(1, NY):
            y_copy(it, s, k).wait_recv()
            total += y_in[it, s, k - 1].astype(f32)
        if s == 0:
            s_in[it, row] = total.astype(bf16)
        else:
            z_out[s] = total.astype(bf16)
            z_copy(it, s).start()

    def prepare():
        for part in range(3):
            turned = contrast_ref[part].T * weight_ref[:, :NT]
            cw_ref[part] = jnp.concatenate([turned, jnp.zeros((NP, TPAD - NT), f32)], axis=1)
        lat[:, NQ * 32 :, :] = jnp.zeros((2, QPAD * 32 - NQ * 32, 128), f32)

    def iteration(it, carry):
        s = 0
        for event in plan:
            if event[0] == "send":
                _, part, rel, way = event
                ring_copy(it, part, rel, way, slot[event[1:]]).start()
            elif event[0] == "recv":
                _, part, rel, way = event
                there = ((rel[0] + STEP[way][0]) % NX, (rel[1] + STEP[way][1]) % NZ)
                ring_copy(it, part, rel, way, slot[(part, there, way)]).wait_recv()
            else:
                multiply(it, s, event[1])
                if s == 0:
                    pl.when(it == 0)(prepare)
                if s >= 3:
                    add_mate(it, s - 3)
                if s >= 7:
                    add_y(it, s - 7)
                s += 1
        for late in range(ROWS, ROWS + 3):
            add_mate(it, late - 3)
            add_y(it, late - 7)
        for late in range(ROWS - 4, ROWS):
            add_y(it, late)
        pl.when(it == 0)(table_copy.wait)
        for s in range(1, ROWS):
            z_arrival(it, s).wait_recv()

        def coefficients(block, window):
            lanes = slice(window * 128, (window + 1) * 128)
            return jnp.concatenate([s_in[it, block, :, lanes], s_in[it, block + 8, :, lanes]], axis=0)

        legendre_in(found, coefficients, w_ref, lat)
        columns(fs_ref, fa_ref, cw_ref, lat, spec)

        def done(k):
            @pl.when(col != k)
            def _():
                b_copy(it, k).start()

        legendre_out(found, w_ref, spec, b_out, done)
        b_in[it, core * NY + y] = b_out[pl.ds(2 * col, 2)]
        for event in plan:
            if event[0] == "send":
                _, part, rel, way = event
                ring_copy(it, part, rel, way, slot[event[1:]]).wait_send()
        for s in range(ROWS):
            mate_copy(it, s).wait_send()
            for k in range(1, NY):
                y_copy(it, s, k).wait_send()
            if s > 0:
                z_copy(it, s).wait_send()
        for k in range(COLS):

            @pl.when(col != k)
            def _():
                b_arrival(it, k).wait_recv()

        for half in range(2):
            rows = slice(half * HALF, (half + 1) * HALF)
            value = jnp.concatenate([b_in[it, k, half].astype(f32) for k in range(COLS)], axis=0)
            value = (value.T[:HALF] + panel_ref[rows].astype(f32)).astype(bf16)

            @pl.when(it == 0)
            def _():
                held[1, row, rows] = value

            @pl.when(it == 1)
            def _():
                out_ref[rows] = value

        for k in range(COLS):

            @pl.when(col != k)
            def _():
                b_copy(it, k).wait_send()

        return carry

    lax.fori_loop(0, ITERS, iteration, 0)


def steps(t, panel, contrast, weight, w, fs, fa, found):
    plan = ring_plan()
    sends = sum(event[0] == "send" for event in plan)
    vmem = pl.BlockSpec(memory_space=pltpu.VMEM)
    dma = pltpu.SemaphoreType.DMA
    bf16, f32 = jnp.bfloat16, jnp.float32
    return pl.pallas_call(
        functools.partial(step_kernel, plan, found),
        out_shape=jax.ShapeDtypeStruct((2 * HALF, 128), bf16),
        in_specs=[vmem] * 4 + [pl.BlockSpec(memory_space=pl.ANY)] + [vmem] * 2,
        out_specs=vmem,
        scratch_shapes=[
            pltpu.VMEM((ITERS, ROWS, 2 * HALF, 128), bf16),
            pltpu.VMEM((4, 128, LANES), f32),
            pltpu.VMEM((ROWS, 64, LANES), bf16),
            pltpu.VMEM((ITERS, ROWS, 64, LANES), bf16),
            pltpu.VMEM((ROWS, 64, LANES), bf16),
            pltpu.VMEM((ITERS, ROWS, NY - 1, PER, LANES), bf16),
            pltpu.VMEM((ROWS, PER, LANES), bf16),
            pltpu.VMEM((ITERS, ROWS, PER, LANES), bf16),
            pltpu.VMEM((ROWS, PER, LANES), bf16),
            pltpu.VMEM((ITERS, COLS, 2, PER, LANES), bf16),
            pltpu.VMEM(w.shape, bf16),
            pltpu.VMEM((3, NP, TPAD), f32),
            pltpu.VMEM((2, QPAD * 32, 128), f32),
            pltpu.VMEM((2, QPAD * 32, 128), f32),
            dma(()),
            dma((sends,)),
            dma((ITERS, sends)),
            dma((ROWS,)),
            dma((ITERS, ROWS)),
            dma((ROWS * 3,)),
            dma((ITERS, ROWS * 3)),
            dma((ROWS,)),
            dma((ITERS, ROWS)),
            dma((COLS,)),
            dma((ITERS, COLS)),
        ],
        compiler_params=pltpu.CompilerParams(
            collective_id=0, has_side_effects=True, vmem_limit_bytes=58 * MIB
        ),
        name="steps",
    )(t, panel, contrast, weight, w, fs, fa)


def body(tmatrix, panel, contrast):
    found, windows, fs, fa, weight = tables()
    t = jnp.stack([tmatrix[:, :BLK], tmatrix[:, BLK:]])
    t = jnp.pad(t, ((0, 0), (0, LANES - BLK), (0, HALF - BLK)))
    pad = jnp.pad(panel.reshape(2, BLK, 128), ((0, 0), (0, HALF - BLK), (0, 0)))
    weight = jnp.asarray(np.pad(weight, (0, TPAD - NT)).reshape(1, TPAD))
    u = steps(
        t,
        pad.reshape(2 * HALF, 128),
        contrast,
        weight,
        jnp.asarray(windows),
        jnp.asarray(fs),
        jnp.asarray(fa),
        found,
    )
    return jnp.concatenate([u[:BLK], u[HALF : HALF + BLK]], axis=0)


def solution(mesh):
    placed = (P("row", "col"), P("col", "row"), P())
    return jax.shard_map(
        body, mesh=mesh, in_specs=placed, out_specs=P("col", "row"), check_vma=False
    )
```

```python
import functools

import jax
import jax.numpy as jnp
import ml_dtypes
import numpy as np
from jax import lax
from jax.experimental import pallas as pl
from jax.experimental.pallas import tpu as pltpu
from jax.sharding import PartitionSpec as P

LDEG = 72
ITERS = 2
NT = 2 * LDEG
NP = 4 * LDEG
NQ = 2 * LDEG + 1
NX = 4
NZ = 4
NY = 4
ROWS = 16
COLS = 8
BLK = 666
HALF = 672
LANES = 768
WIN = LANES // 128
TPAD = 256
QPAD = 160
PHASES = 2 * ITERS
PER = 8
CC = 2 * PER
STEPS = ROWS // 2
MIB = 1024 * 1024
MESH = pl.DeviceIdType.MESH


def angular_tables(degree):
    lat_count = 2 * degree
    lon_count = 4 * degree
    freq_count = 2 * degree + 1
    colatitude = (np.arange(lat_count) + 0.5) * np.pi / lat_count
    cos_col = np.cos(colatitude)
    sin_col = np.sin(colatitude)
    legendre = np.zeros((freq_count, degree, lat_count))
    diagonal_term = np.full(lat_count, np.sqrt(0.5))
    for order_m in range(degree + 1):
        if order_m > 0:
            diagonal_term = (
                diagonal_term * np.sqrt((2.0 * order_m + 1.0) / (2.0 * order_m)) * sin_col
            )
        earlier = np.zeros(lat_count)
        latest = diagonal_term
        for degree_l in range(order_m, degree + 1):
            if degree_l == order_m:
                current = diagonal_term
            elif degree_l == order_m + 1:
                current = np.sqrt(2.0 * order_m + 3.0) * cos_col * diagonal_term
            else:
                factor_a = np.sqrt((4.0 * degree_l**2 - 1.0) / (degree_l**2 - order_m**2))
                factor_b = np.sqrt(
                    ((degree_l - 1.0) ** 2 - order_m**2) / (4.0 * (degree_l - 1.0) ** 2 - 1.0)
                )
                current = factor_a * (cos_col * latest - factor_b * earlier)
            if degree_l > order_m:
                earlier, latest = (latest, current)
            if degree_l >= 1:
                legendre[order_m, degree_l - 1] = current
                if order_m >= 1:
                    legendre[degree + order_m, degree_l - 1] = current
    longitude = 2.0 * np.pi * np.arange(lon_count) / lon_count
    fourier = np.zeros((freq_count, lon_count))
    fourier[0] = 1.0 / np.sqrt(2.0 * np.pi)
    for order_m in range(1, degree + 1):
        fourier[order_m] = np.cos(order_m * longitude) / np.sqrt(np.pi)
        fourier[degree + order_m] = np.sin(order_m * longitude) / np.sqrt(np.pi)
    weight = sin_col * (np.pi / lat_count) * (2.0 * np.pi / lon_count)
    return (legendre, fourier, weight)


def meetings():
    owner = []
    for q in range(NQ):
        m = q if q <= LDEG else q - LDEG
        owner += [(q, l) for l in range(max(m, 1), LDEG + 1)]
    found = []
    for block in range(ROWS // 2):
        for window in range(WIN):
            first = block * BLK + window * 128
            last = min(first + 128, (block + 1) * BLK)
            for q in sorted({owner[n][0] for n in range(first, last)}):
                rows = [(n - first, owner[n][1] - 1) for n in range(first, last) if owner[n][0] == q]
                found.append((block, window, q, rows))
    return found


def split(table):
    high = table.astype(np.float32).astype(ml_dtypes.bfloat16)
    low = (table - high.astype(np.float64)).astype(np.float32).astype(ml_dtypes.bfloat16)
    return np.stack([high, low])


@functools.lru_cache(None)
def tables():
    legendre, fourier, weight = angular_tables(LDEG)
    found = meetings()
    windows = np.zeros((len(found), 128, TPAD))
    for index, (block, window, q, rows) in enumerate(found):
        for place, level in rows:
            windows[index, place, :NT] = legendre[q, level]
    padded = np.zeros((QPAD, NP))
    padded[:NQ] = fourier
    return (
        [f[:3] for f in found],
        windows.astype(np.float32).astype(ml_dtypes.bfloat16),
        split(np.ascontiguousarray(padded.T)),
        split(padded),
        weight.astype(np.float32),
    )


def dot(a, b):
    return jnp.dot(a, b, preferred_element_type=jnp.float32)


def two(value):
    high = value.astype(jnp.bfloat16)
    return high, (value - high.astype(jnp.float32)).astype(jnp.bfloat16)


def legendre_in(found, coefficients, w_ref, lat):
    by_q = {}
    for index, (block, window, q) in enumerate(found):
        by_q.setdefault(q, []).append((index, block, window))
    for q in range(NQ):
        total = None
        for index, block, window in by_q[q]:
            term = dot(coefficients(block, window), w_ref[index])
            total = term if total is None else total + term
        for half in range(2):
            lat[half, q * CC : (q + 1) * CC, :] = total[:, half * 128 : half * 128 + 128]


def columns(some, fs_ref, fa_ref, cw_ref, lat, spec):
    def synthesis(place):
        rows = pl.ds(place, QPAD, stride=CC)
        high, low = two(jnp.concatenate([lat[0, rows, :], lat[1, rows, :]], axis=1))
        return dot(fs_ref[0], high) + dot(fs_ref[1], high) + dot(fs_ref[0], low)

    def analysis(place, value):
        high, low = two(value)
        value = dot(fa_ref[0], high) + dot(fa_ref[1], high) + dot(fa_ref[0], low)
        for half in range(2):
            spec[half, pl.ds(place, QPAD, stride=CC), :] = value[:, half * 128 : half * 128 + 128]

    for k in some:
        first = synthesis(k)
        second = synthesis(PER + k)
        analysis(k, cw_ref[0] * first + cw_ref[1] * second)
        analysis(PER + k, cw_ref[1] * first + cw_ref[2] * second)


def legendre_out(found, pair, w_ref, spec, b_ref):
    by_window = {}
    for index, (block, window, q) in enumerate(found):
        by_window.setdefault((block, window), []).append((index, q))
    for window in range(WIN):
        values = []
        for block in (2 * pair, 2 * pair + 1):
            total = None
            for index, q in by_window[block, window]:
                rows = slice(q * CC, (q + 1) * CC)
                high, low = two(jnp.concatenate([spec[0, rows, :], spec[1, rows, :]], axis=1))
                term = lax.dot_general(
                    jnp.concatenate([high, low], axis=0),
                    w_ref[index],
                    (((1,), (1,)), ((), ())),
                    preferred_element_type=jnp.float32,
                )
                total = term if total is None else total + term
            values.append(total[:CC] + total[CC:])
        lanes = slice(window * 128, (window + 1) * 128)
        for c in range(2):
            part = [value[c * PER : (c + 1) * PER] for value in values]
            b_ref[pair + 4 * c, :, lanes] = jnp.concatenate(part, axis=0).astype(jnp.bfloat16)


STEP = {"x+": (1, 0), "x-": (-1, 0), "z+": (0, 1), "z-": (0, -1)}
A, A0, A1 = (0, 336), (0, 176), (176, 160)
B, B0, B1 = (336, 336), (336, 176), (512, 160)


def ring_plan():
    plan = []

    def send(part, rel, way):
        plan.append(("send", part, (rel[0] % NX, rel[1] % NZ), way))

    def recv(part, rel, way):
        plan.append(("recv", part, (rel[0] % NX, rel[1] % NZ), way))

    def use(*rels):
        for rel in rels:
            plan.append(("use", (rel[0] % NX, rel[1] % NZ)))

    own = (0, 0)
    for way in ("x+", "x-"):
        send(A, own, way)
    for way in ("z+", "z-"):
        send(B, own, way)
    for way in ("z+", "z-"):
        send(A, own, way)
    for way in ("x+", "x-"):
        send(B, own, way)
    use(own)
    for part, quart, rel, way in ((A, A0, (-1, 0), "x+"), (A, A1, (1, 0), "x-")):
        recv(part, rel, way)
        send(quart, rel, way)
        send(A, rel, "z+")
        send(A, rel, "z-")
    for part, quart, rel, way in ((B, B0, (0, -1), "z+"), (B, B1, (0, 1), "z-")):
        recv(part, rel, way)
        send(quart, rel, way)
        send(B, rel, "x+")
        send(B, rel, "x-")
    for quart, rel, way in ((A0, (0, -1), "z+"), (A1, (0, 1), "z-")):
        recv(A, rel, way)
        send(quart, rel, way)
    for quart, rel, way in ((B0, (-1, 0), "x+"), (B1, (1, 0), "x-")):
        recv(B, rel, way)
        send(quart, rel, way)
    use((-1, 0), (1, 0))
    recv(A0, (2, 0), "x+")
    recv(A1, (2, 0), "x-")
    send(A, (2, 0), "z+")
    send(A, (2, 0), "z-")
    recv(B0, (0, 2), "z+")
    recv(B1, (0, 2), "z-")
    send(B, (0, 2), "x+")
    send(B, (0, 2), "x-")
    use((0, -1), (0, 1))
    for x in (-1, 1):
        for quart, z, way in ((A0, -1, "z+"), (A1, 1, "z-")):
            recv(A, (x, z), way)
            send(quart, (x, z), way)
    for z in (-1, 1):
        for quart, x, way in ((B0, -1, "x+"), (B1, 1, "x-")):
            recv(B, (x, z), way)
            send(quart, (x, z), way)
    use((-1, -1), (-1, 1))
    recv(A0, (0, 2), "z+")
    recv(A1, (0, 2), "z-")
    recv(B0, (2, 0), "x+")
    recv(B1, (2, 0), "x-")
    for quart, z, way in ((A0, -1, "z+"), (A1, 1, "z-")):
        recv(A, (2, z), way)
        send(quart, (2, z), way)
    for quart, x, way in ((B0, -1, "x+"), (B1, 1, "x-")):
        recv(B, (x, 2), way)
        send(quart, (x, 2), way)
    use((1, -1), (1, 1), (0, 2), (2, 0))
    for x in (-1, 1):
        recv(A0, (x, 2), "z+")
        recv(A1, (x, 2), "z-")
        use((x, 2))
    for z in (-1, 1):
        recv(B0, (2, z), "x+")
        recv(B1, (2, z), "x-")
        use((2, z))
    recv(A0, (2, 2), "z+")
    recv(A1, (2, 2), "z-")
    recv(B0, (2, 2), "x+")
    recv(B1, (2, 2), "x-")
    use((2, 2))
    return plan


def greet(others):
    barrier = pltpu.get_barrier_semaphore()
    for other in others:
        pl.semaphore_signal(barrier, inc=1, device_id=other, device_id_type=MESH)
    pl.semaphore_wait(barrier, len(others))


def step_kernel(
    plan,
    found,
    t_ref,
    panel_ref,
    contrast_ref,
    weight_ref,
    w_hbm,
    fs_ref,
    fa_ref,
    out_ref,
    held,
    prod,
    mate_out,
    mate_in,
    sums,
    y_in,
    z_out,
    s_in,
    b_out,
    b_in,
    w_ref,
    cw_ref,
    lat,
    spec,
    w_sem,
    ring_send,
    ring_recv,
    mate_send,
    mate_recv,
    y_send,
    y_recv,
    z_send,
    z_recv,
    b_send,
    b_recv,
):
    row = lax.axis_index("row")
    col = lax.axis_index("col")
    x, z = row // NZ, row % NZ
    y, core = col // 2, col % 2
    f32, bf16 = jnp.float32, jnp.bfloat16

    def block_of(rel):
        return ((x + rel[0] + NX) % NX) * NZ + (z + rel[1] + NZ) % NZ

    table_copy = pltpu.make_async_copy(w_hbm, w_ref, w_sem)
    table_copy.start()
    for phase in range(2):
        held[phase, row] = panel_ref[phase]
    greet(
        [{"row": (row + k) % ROWS} for k in range(1, ROWS)]
        + [{"col": (col + k) % COLS} for k in range(1, COLS)]
    )
    mate = {"col": y * 2 + (1 - core)}
    y_peers = [{"col": ((y + k) % NY) * 2 + core} for k in range(1, NY)]

    slot = {}
    for event in plan:
        if event[0] == "send":
            slot[event[1:]] = len(slot)
    order = [event[1] for event in plan if event[0] == "use"]

    def ring_copy(it, part, rel, way, number):
        here = held.at[it, block_of(rel), pl.ds(part[0], part[1])]
        return pltpu.make_async_remote_copy(
            src_ref=here,
            dst_ref=here,
            send_sem=ring_send.at[it % 2, number],
            recv_sem=ring_recv.at[it, number],
            device_id={"row": block_of(STEP[way])},
            device_id_type=MESH,
        )

    def mate_copy(it, s):
        return pltpu.make_async_remote_copy(
            src_ref=mate_out.at[s],
            dst_ref=mate_in.at[it, s],
            send_sem=mate_send.at[s],
            recv_sem=mate_recv.at[it, s],
            device_id=mate,
            device_id_type=MESH,
        )

    def y_copy(it, s, k):
        to = (y + k) % NY
        number = s * 3 + k - 1
        return pltpu.make_async_remote_copy(
            src_ref=sums.at[s, pl.ds(pl.multiple_of(to * CC, CC), CC)],
            dst_ref=y_in.at[it, s, k - 1],
            send_sem=y_send.at[number],
            recv_sem=y_recv.at[it, number],
            device_id=y_peers[k - 1],
            device_id_type=MESH,
        )

    def z_copy(it, s):
        return pltpu.make_async_remote_copy(
            src_ref=z_out.at[s],
            dst_ref=s_in.at[it, row],
            send_sem=z_send.at[s],
            recv_sem=z_recv.at[it, s],
            device_id={"row": block_of(order[s])},
            device_id_type=MESH,
        )

    def z_arrival(it, s):
        back = (-order[s][0], -order[s][1])
        return pltpu.make_async_remote_copy(
            src_ref=z_out.at[s],
            dst_ref=s_in.at[it, block_of(back)],
            send_sem=z_send.at[s],
            recv_sem=z_recv.at[it, s],
            device_id={"row": block_of(back)},
            device_id_type=MESH,
        )

    def b_copy(it, k):
        return pltpu.make_async_remote_copy(
            src_ref=b_out.at[k],
            dst_ref=b_in.at[it, core * NY + y],
            send_sem=b_send.at[k],
            recv_sem=b_recv.at[it, col],
            device_id={"col": k},
            device_id_type=MESH,
        )

    def b_arrival(it, k):
        return pltpu.make_async_remote_copy(
            src_ref=b_out.at[k],
            dst_ref=b_in.at[it, k % 2 * NY + k // 2],
            send_sem=b_send.at[k],
            recv_sem=b_recv.at[it, k],
            device_id={"col": k},
            device_id_type=MESH,
        )

    def multiply(it, s):
        first, second = [block_of(rel) for rel in order[2 * s : 2 * s + 2]]
        here = s % 2
        one, other = held[it, first], held[it, second]
        lower = jnp.concatenate([one[:, :64], other[:, :64]], axis=1)
        upper = jnp.concatenate([one[:, 64:], other[:, 64:]], axis=1)
        for chunk in range(LANES // 256):
            rows = slice(chunk * 256, (chunk + 1) * 256)
            prod[here, :, rows] = (dot(t_ref[0, rows], lower) + dot(t_ref[1, rows], upper)).T
        mate_out[s] = core_rows(here, 1 - core).astype(bf16)
        mate_copy(it, s).start()

    def core_rows(here, which):
        start = pl.multiple_of(which * 32, 32)
        return jnp.concatenate([prod[here, pl.ds(start, 32), :], prod[here, pl.ds(64 + start, 32), :]], axis=0)

    def add_mate(it, s):
        mate_copy(it, s).wait_recv()
        value = core_rows(s % 2, core) + mate_in[it, s].astype(f32)
        for owner in range(NY):
            part = [value[k * 32 + owner * PER : k * 32 + (owner + 1) * PER] for k in range(2)]
            sums[s, owner * CC : (owner + 1) * CC, :] = jnp.concatenate(part, axis=0).astype(bf16)
        for k in (2, 1, 3):
            y_copy(it, s, k).start()

    def add_y(it, s):
        total = sums[s, pl.ds(pl.multiple_of(y * CC, CC), CC)].astype(f32)
        for k in range(1, NY):
            y_copy(it, s, k).wait_recv()
            total += y_in[it, s, k - 1].astype(f32)
        for k in range(2):
            part = total[k * PER : (k + 1) * PER]
            folded = jnp.concatenate([part[:, : LANES // 2], part[:, LANES // 2 :]], axis=0).astype(bf16)
            if s == 0 and k == 0:
                s_in[it, row] = folded
            else:
                z_out[2 * s + k] = folded
                z_copy(it, 2 * s + k).start()

    def prepare():
        for part in range(3):
            turned = contrast_ref[part].T * weight_ref[:, :NT]
            cw_ref[part] = jnp.concatenate([turned, jnp.zeros((NP, TPAD - NT), f32)], axis=1)
        lat[:, NQ * CC :, :] = jnp.zeros((2, (QPAD - NQ) * CC, 128), f32)

    def own_sends(it):
        for event in plan:
            if event[0] == "send" and event[2] == (0, 0):
                _, part, rel, way = event
                ring_copy(it, part, rel, way, slot[event[1:]]).start()

    def gathering(it):
        groups, events, uses = [], [], 0
        for event in plan:
            if event[0] == "use":
                uses += 1
                if uses % 2 == 0:
                    groups.append(events)
                    events = []
            elif event[0] == "recv" or event[2] != (0, 0):
                events.append(event)

        def ticks(s):
            if s < STEPS:
                for kind, part, rel, way in groups[s]:
                    if kind == "send":
                        ring_copy(it, part, rel, way, slot[(part, rel, way)]).start()
                    else:
                        there = ((rel[0] + STEP[way][0]) % NX, (rel[1] + STEP[way][1]) % NZ)
                        ring_copy(it, part, rel, way, slot[(part, there, way)]).wait_recv()
                multiply(it, s)
            if 0 <= s - 1 < STEPS:
                add_mate(it, s - 1)
            if 0 <= s - 3 < STEPS:
                add_y(it, s - 3)

        return [functools.partial(ticks, s) for s in range(STEPS + 3)]

    def sent(it):
        for event in plan:
            if event[0] == "send":
                _, part, rel, way = event
                ring_copy(it, part, rel, way, slot[event[1:]]).wait_send()
        for s in range(STEPS):
            mate_copy(it, s).wait_send()
            for k in range(1, NY):
                y_copy(it, s, k).wait_send()
        for s in range(1, ROWS):
            z_copy(it, s).wait_send()

    def couple(it, ticks):
        ticks = list(ticks)

        def tick(count):
            for _ in range(count):
                if ticks:
                    ticks.pop(0)()

        for s in range(1, ROWS):
            z_arrival(it, s).wait_recv()

        def coefficients(block, window):
            low = window % 3 * 128
            lanes = slice(low, low + 128)
            rows = slice(window // 3 * PER, (window // 3 + 1) * PER)
            both = [s_in[it, b, :, lanes].astype(f32)[rows] for b in (block, block + 8)]
            return jnp.concatenate(both, axis=0).astype(bf16)

        tick(1)
        legendre_in(found, coefficients, w_ref, lat)
        tick(1)
        for k in range(0, PER, 2):
            columns((k, k + 1), fs_ref, fa_ref, cw_ref, lat, spec)
            tick(2)
        for pair in range(4):
            legendre_out(found, pair, w_ref, spec, b_out)
            for k in (pair, pair + 4):

                @pl.when(col != k)
                def _():
                    b_copy(it, k).start()

            tick(1)
        b_in[it, core * NY + y] = b_out[col]
        tick(len(ticks))

    def come_back(it):
        for k in range(COLS):

            @pl.when(col != k)
            def _():
                b_arrival(it, k).wait_recv()

        came = [b_in[it, k].astype(f32) for k in range(COLS)]
        value = jnp.concatenate([c[:PER] for c in came] + [c[PER:] for c in came], axis=0)
        return (value.T[:HALF] + panel_ref[it % 2].astype(f32)).astype(bf16)

    def returned(it):
        for k in range(COLS):

            @pl.when(col != k)
            def _():
                b_copy(it, k).wait_send()

    own_sends(0)
    for s, tick in enumerate(gathering(0)):
        tick()
        if s == 0:
            prepare()
        if s == STEPS - 1:
            own_sends(1)
    sent(0)
    table_copy.wait()

    def phase(it, carry):
        couple(it, gathering(it + 1))
        value = come_back(it)

        @pl.when(it < PHASES - 2)
        def _():
            held[it + 2, row] = value
            own_sends(it + 2)

        @pl.when(it == PHASES - 2)
        def _():
            out_ref[0] = value

        returned(it)
        sent(it + 1)
        return carry

    lax.fori_loop(0, PHASES - 1, phase, 0)
    couple(PHASES - 1, [])
    out_ref[1] = come_back(PHASES - 1)
    returned(PHASES - 1)


def steps(t, panel, contrast, weight, w, fs, fa, found):
    plan = ring_plan()
    sends = sum(event[0] == "send" for event in plan)
    vmem = pl.BlockSpec(memory_space=pltpu.VMEM)
    dma = pltpu.SemaphoreType.DMA
    bf16, f32 = jnp.bfloat16, jnp.float32
    return pl.pallas_call(
        functools.partial(step_kernel, plan, found),
        out_shape=jax.ShapeDtypeStruct((2, HALF, 128), bf16),
        in_specs=[vmem] * 4 + [pl.BlockSpec(memory_space=pl.ANY)] + [vmem] * 2,
        out_specs=vmem,
        scratch_shapes=[
            pltpu.VMEM((PHASES, ROWS, HALF, 128), bf16),
            pltpu.VMEM((2, 128, LANES), f32),
            pltpu.VMEM((STEPS, 64, LANES), bf16),
            pltpu.VMEM((PHASES, STEPS, 64, LANES), bf16),
            pltpu.VMEM((STEPS, 64, LANES), bf16),
            pltpu.VMEM((PHASES, STEPS, NY - 1, CC, LANES), bf16),
            pltpu.VMEM((ROWS, CC, LANES // 2), bf16),
            pltpu.VMEM((PHASES, ROWS, CC, LANES // 2), bf16),
            pltpu.VMEM((COLS, CC, LANES), bf16),
            pltpu.VMEM((PHASES, COLS, CC, LANES), bf16),
            pltpu.VMEM(w.shape, bf16),
            pltpu.VMEM((3, NP, TPAD), f32),
            pltpu.VMEM((2, QPAD * CC, 128), f32),
            pltpu.VMEM((2, QPAD * CC, 128), f32),
            dma(()),
            dma((2, sends)),
            dma((PHASES, sends)),
            dma((STEPS,)),
            dma((PHASES, STEPS)),
            dma((STEPS * 3,)),
            dma((PHASES, STEPS * 3)),
            dma((ROWS,)),
            dma((PHASES, ROWS)),
            dma((COLS,)),
            dma((PHASES, COLS)),
        ],
        compiler_params=pltpu.CompilerParams(
            collective_id=0, has_side_effects=True, vmem_limit_bytes=58 * MIB
        ),
        name="steps",
    )(t, panel, contrast, weight, w, fs, fa)


def body(tmatrix, panel, contrast):
    found, windows, fs, fa, weight = tables()
    t = jnp.stack([tmatrix[:, :BLK], tmatrix[:, BLK:]])
    t = jnp.pad(t, ((0, 0), (0, LANES - BLK), (0, HALF - BLK)))
    pad = panel.reshape(2, BLK, 2, 64).transpose(2, 1, 0, 3).reshape(2, BLK, 128)
    pad = jnp.pad(pad, ((0, 0), (0, HALF - BLK), (0, 0)))
    weight = jnp.asarray(np.pad(weight, (0, TPAD - NT)).reshape(1, TPAD))
    u = steps(
        t,
        pad,
        contrast,
        weight,
        jnp.asarray(windows),
        jnp.asarray(fs),
        jnp.asarray(fa),
        found,
    )
    return u[:, :BLK].reshape(2, BLK, 2, 64).transpose(2, 1, 0, 3).reshape(2 * BLK, 128)


def solution(mesh):
    placed = (P("row", "col"), P("col", "row"), P())
    return jax.shard_map(
        body, mesh=mesh, in_specs=placed, out_specs=P("col", "row"), check_vma=False
    )
```

```python
import functools

import jax
import jax.numpy as jnp
import ml_dtypes
import numpy as np
from jax import lax
from jax.experimental import pallas as pl
from jax.experimental.pallas import tpu as pltpu
from jax.sharding import PartitionSpec as P

LDEG = 72
ITERS = 2
NT = 2 * LDEG
NP = 4 * LDEG
NQ = 2 * LDEG + 1
NX = 4
NZ = 4
NY = 4
ROWS = 16
COLS = 8
BLK = 666
HALF = 672
QUART = HALF // 2
LANES = 768
WIN = LANES // 128
TPAD = 256
KPAD = 1408
QPAD = 160
PER = 16
MIB = 1024 * 1024
MESH = pl.DeviceIdType.MESH


def angular_tables(degree):
    lat_count = 2 * degree
    lon_count = 4 * degree
    freq_count = 2 * degree + 1
    colatitude = (np.arange(lat_count) + 0.5) * np.pi / lat_count
    cos_col = np.cos(colatitude)
    sin_col = np.sin(colatitude)
    legendre = np.zeros((freq_count, degree, lat_count))
    diagonal_term = np.full(lat_count, np.sqrt(0.5))
    for order_m in range(degree + 1):
        if order_m > 0:
            diagonal_term = (
                diagonal_term * np.sqrt((2.0 * order_m + 1.0) / (2.0 * order_m)) * sin_col
            )
        earlier = np.zeros(lat_count)
        latest = diagonal_term
        for degree_l in range(order_m, degree + 1):
            if degree_l == order_m:
                current = diagonal_term
            elif degree_l == order_m + 1:
                current = np.sqrt(2.0 * order_m + 3.0) * cos_col * diagonal_term
            else:
                factor_a = np.sqrt((4.0 * degree_l**2 - 1.0) / (degree_l**2 - order_m**2))
                factor_b = np.sqrt(
                    ((degree_l - 1.0) ** 2 - order_m**2) / (4.0 * (degree_l - 1.0) ** 2 - 1.0)
                )
                current = factor_a * (cos_col * latest - factor_b * earlier)
            if degree_l > order_m:
                earlier, latest = (latest, current)
            if degree_l >= 1:
                legendre[order_m, degree_l - 1] = current
                if order_m >= 1:
                    legendre[degree + order_m, degree_l - 1] = current
    longitude = 2.0 * np.pi * np.arange(lon_count) / lon_count
    fourier = np.zeros((freq_count, lon_count))
    fourier[0] = 1.0 / np.sqrt(2.0 * np.pi)
    for order_m in range(1, degree + 1):
        fourier[order_m] = np.cos(order_m * longitude) / np.sqrt(np.pi)
        fourier[degree + order_m] = np.sin(order_m * longitude) / np.sqrt(np.pi)
    weight = sin_col * (np.pi / lat_count) * (2.0 * np.pi / lon_count)
    return (legendre, fourier, weight)


def meetings():
    owner = []
    for q in range(NQ):
        m = q if q <= LDEG else q - LDEG
        owner += [(q, l) for l in range(max(m, 1), LDEG + 1)]
    found = []
    for block in range(ROWS // 2):
        for window in range(WIN):
            first = block * BLK + window * 128
            last = min(first + 128, (block + 1) * BLK)
            for q in sorted({owner[n][0] for n in range(first, last)}):
                rows = [(n - first, owner[n][1] - 1) for n in range(first, last) if owner[n][0] == q]
                found.append((block, window, q, rows))
    return found


def split(table):
    high = table.astype(np.float32).astype(ml_dtypes.bfloat16)
    low = (table - high.astype(np.float64)).astype(np.float32).astype(ml_dtypes.bfloat16)
    return np.stack([high, low])


@functools.lru_cache(None)
def tables():
    legendre, fourier, weight = angular_tables(LDEG)
    found = meetings()
    windows = np.zeros((len(found), 128, TPAD))
    for index, (block, window, q, rows) in enumerate(found):
        for place, level in rows:
            windows[index, place, :NT] = legendre[q, level]
    padded = np.zeros((QPAD, NP))
    padded[:NQ] = fourier
    return (
        [f[:3] for f in found],
        windows.astype(np.float32).astype(ml_dtypes.bfloat16),
        split(np.ascontiguousarray(padded.T)),
        split(padded),
        weight.astype(np.float32),
    )


def dot(a, b):
    return jnp.dot(a, b, preferred_element_type=jnp.float32)


def two(value):
    high = value.astype(jnp.bfloat16)
    return high, (value - high.astype(jnp.float32)).astype(jnp.bfloat16)


def legendre_in(found, coefficients, w_ref, lat):
    by_q = {}
    for index, (block, window, q) in enumerate(found):
        by_q.setdefault(q, []).append((index, block, window))
    for q in range(NQ):
        total = None
        for index, block, window in by_q[q]:
            term = dot(coefficients(block, window), w_ref[index])
            total = term if total is None else total + term
        for half in range(2):
            lat[half, q * 32 : (q + 1) * 32, :] = total[:, half * 128 : half * 128 + 128]


def columns(fs_ref, fa_ref, cw_ref, lat, spec):
    def synthesis(place):
        rows = pl.ds(place, QPAD, stride=32)
        high, low = two(jnp.concatenate([lat[0, rows, :], lat[1, rows, :]], axis=1))
        return dot(fs_ref[0], high) + dot(fs_ref[1], high) + dot(fs_ref[0], low)

    def analysis(place, value):
        high, low = two(value)
        value = dot(fa_ref[0], high) + dot(fa_ref[1], high) + dot(fa_ref[0], low)
        for half in range(2):
            spec[half, pl.ds(place, QPAD, stride=32), :] = value[:, half * 128 : half * 128 + 128]

    def column(k, carry):
        first = synthesis(k)
        second = synthesis(PER + k)
        analysis(k, cw_ref[0] * first + cw_ref[1] * second)
        analysis(PER + k, cw_ref[1] * first + cw_ref[2] * second)
        return carry

    lax.fori_loop(0, PER, column, 0, unroll=4)


def legendre_out(found, w_ref, spec, b_ref, done):
    by_window = {}
    for index, (block, window, q) in enumerate(found):
        by_window.setdefault((block, window), []).append((index, q))
    for (block, window), members in sorted(by_window.items()):
        total = None
        for index, q in members:
            rows = slice(q * 32, (q + 1) * 32)
            high, low = two(jnp.concatenate([spec[0, rows, :], spec[1, rows, :]], axis=1))
            term = lax.dot_general(
                jnp.concatenate([high, low], axis=0),
                w_ref[index],
                (((1,), (1,)), ((), ())),
                preferred_element_type=jnp.float32,
            )
            total = term if total is None else total + term
        value = (total[:32] + total[32:]).astype(jnp.bfloat16)
        lanes = slice(window * 128, (window + 1) * 128)
        b_ref[block, :, lanes] = value[:PER]
        b_ref[block + 8, :, lanes] = value[PER:]
        if window == WIN - 1 and block % 2 == 1:
            done(block // 2)
            done(block // 2 + 4)


STEP = {"x+": (1, 0), "x-": (-1, 0), "z+": (0, 1), "z-": (0, -1)}
ALL = (0, 2 * HALF)
A = (0, HALF)
B = (HALF, HALF)
A0, A1 = (0, QUART), (QUART, QUART)
B0, B1 = (HALF, QUART), (HALF + QUART, QUART)


def ring_plan():
    plan = []

    def send(part, rel, way):
        plan.append(("send", part, (rel[0] % NX, rel[1] % NZ), way))

    def recv(part, rel, way):
        plan.append(("recv", part, (rel[0] % NX, rel[1] % NZ), way))

    def use(*rels):
        for rel in rels:
            plan.append(("use", (rel[0] % NX, rel[1] % NZ)))

    own = (0, 0)
    for way in ("x+", "x-"):
        send(A, own, way)
    for way in ("z+", "z-"):
        send(B, own, way)
    for way in ("z+", "z-"):
        send(A, own, way)
    for way in ("x+", "x-"):
        send(B, own, way)
    use(own)
    for part, quart, rel, way in ((A, A0, (-1, 0), "x+"), (A, A1, (1, 0), "x-")):
        recv(part, rel, way)
        send(quart, rel, way)
        send(A, rel, "z+")
        send(A, rel, "z-")
    for part, quart, rel, way in ((B, B0, (0, -1), "z+"), (B, B1, (0, 1), "z-")):
        recv(part, rel, way)
        send(quart, rel, way)
        send(B, rel, "x+")
        send(B, rel, "x-")
    for quart, rel, way in ((A0, (0, -1), "z+"), (A1, (0, 1), "z-")):
        recv(A, rel, way)
        send(quart, rel, way)
    for quart, rel, way in ((B0, (-1, 0), "x+"), (B1, (1, 0), "x-")):
        recv(B, rel, way)
        send(quart, rel, way)
    use((-1, 0), (1, 0))
    recv(A0, (2, 0), "x+")
    recv(A1, (2, 0), "x-")
    send(A, (2, 0), "z+")
    send(A, (2, 0), "z-")
    recv(B0, (0, 2), "z+")
    recv(B1, (0, 2), "z-")
    send(B, (0, 2), "x+")
    send(B, (0, 2), "x-")
    use((0, -1), (0, 1))
    for x in (-1, 1):
        for quart, z, way in ((A0, -1, "z+"), (A1, 1, "z-")):
            recv(A, (x, z), way)
            send(quart, (x, z), way)
    for z in (-1, 1):
        for quart, x, way in ((B0, -1, "x+"), (B1, 1, "x-")):
            recv(B, (x, z), way)
            send(quart, (x, z), way)
    use((-1, -1), (-1, 1))
    recv(A0, (0, 2), "z+")
    recv(A1, (0, 2), "z-")
    recv(B0, (2, 0), "x+")
    recv(B1, (2, 0), "x-")
    for quart, z, way in ((A0, -1, "z+"), (A1, 1, "z-")):
        recv(A, (2, z), way)
        send(quart, (2, z), way)
    for quart, x, way in ((B0, -1, "x+"), (B1, 1, "x-")):
        recv(B, (x, 2), way)
        send(quart, (x, 2), way)
    use((1, -1), (1, 1), (0, 2), (2, 0))
    for x in (-1, 1):
        recv(A0, (x, 2), "z+")
        recv(A1, (x, 2), "z-")
        use((x, 2))
    for z in (-1, 1):
        recv(B0, (2, z), "x+")
        recv(B1, (2, z), "x-")
        use((2, z))
    recv(A0, (2, 2), "z+")
    recv(A1, (2, 2), "z-")
    recv(B0, (2, 2), "x+")
    recv(B1, (2, 2), "x-")
    use((2, 2))
    return plan


def greet(others):
    barrier = pltpu.get_barrier_semaphore()
    for other in others:
        pl.semaphore_signal(barrier, inc=1, device_id=other, device_id_type=MESH)
    pl.semaphore_wait(barrier, len(others))


def step_kernel(
    plan,
    found,
    t_ref,
    panel_ref,
    contrast_ref,
    weight_ref,
    w_hbm,
    fs_ref,
    fa_ref,
    out_ref,
    held,
    prod,
    mate_out,
    mate_in,
    sums,
    y_in,
    z_out,
    s_in,
    b_out,
    b_in,
    t_pad,
    w_ref,
    cw_ref,
    lat,
    spec,
    w_sem,
    ring_send,
    ring_recv,
    mate_send,
    mate_recv,
    y_send,
    y_recv,
    z_send,
    z_recv,
    b_send,
    b_recv,
):
    row = lax.axis_index("row")
    col = lax.axis_index("col")
    x, z = row // NZ, row % NZ
    y, core = col // 2, col % 2
    f32, bf16 = jnp.float32, jnp.bfloat16

    def block_of(rel):
        return ((x + rel[0] + NX) % NX) * NZ + (z + rel[1] + NZ) % NZ

    table_copy = pltpu.make_async_copy(w_hbm, w_ref, w_sem)
    table_copy.start()
    for first in range(ITERS):
        held[first, row, 2 * HALF - 16 :] = jnp.zeros((16, 128), bf16)
    held[0, row, : 2 * BLK] = panel_ref[...]
    greet(
        [{"row": (row + k) % ROWS} for k in range(1, ROWS)]
        + [{"col": (col + k) % COLS} for k in range(1, COLS)]
    )
    mate = {"col": y * 2 + (1 - core)}
    y_peers = [{"col": ((y + k) % NY) * 2 + core} for k in range(1, NY)]

    slot = {}
    for event in plan:
        if event[0] == "send":
            slot[event[1:]] = len(slot)
    order = [event[1] for event in plan if event[0] == "use"]

    def ring_copy(it, part, rel, way, number):
        here = held.at[it, block_of(rel), pl.ds(part[0], part[1])]
        return pltpu.make_async_remote_copy(
            src_ref=here,
            dst_ref=here,
            send_sem=ring_send.at[number],
            recv_sem=ring_recv.at[it, number],
            device_id={"row": block_of(STEP[way])},
            device_id_type=MESH,
        )

    def mate_copy(it, s):
        return pltpu.make_async_remote_copy(
            src_ref=mate_out.at[s],
            dst_ref=mate_in.at[it, s],
            send_sem=mate_send.at[s],
            recv_sem=mate_recv.at[it, s],
            device_id=mate,
            device_id_type=MESH,
        )

    def y_copy(it, s, k):
        to = (y + k) % NY
        number = s * 3 + k - 1
        return pltpu.make_async_remote_copy(
            src_ref=sums.at[s, pl.ds(pl.multiple_of(to * PER, PER), PER)],
            dst_ref=y_in.at[it, s, k - 1],
            send_sem=y_send.at[number],
            recv_sem=y_recv.at[it, number],
            device_id=y_peers[k - 1],
            device_id_type=MESH,
        )

    def z_copy(it, s):
        return pltpu.make_async_remote_copy(
            src_ref=z_out.at[s],
            dst_ref=s_in.at[it, row],
            send_sem=z_send.at[s],
            recv_sem=z_recv.at[it, s],
            device_id={"row": block_of(order[s])},
            device_id_type=MESH,
        )

    def z_arrival(it, s):
        back = (-order[s][0], -order[s][1])
        return pltpu.make_async_remote_copy(
            src_ref=z_out.at[s],
            dst_ref=s_in.at[it, block_of(back)],
            send_sem=z_send.at[s],
            recv_sem=z_recv.at[it, s],
            device_id={"row": block_of(back)},
            device_id_type=MESH,
        )

    def b_copy(it, k):
        return pltpu.make_async_remote_copy(
            src_ref=b_out.at[pl.ds(2 * k, 2)],
            dst_ref=b_in.at[it, core * NY + y],
            send_sem=b_send.at[k],
            recv_sem=b_recv.at[it, col],
            device_id={"col": k},
            device_id_type=MESH,
        )

    def b_arrival(it, k):
        return pltpu.make_async_remote_copy(
            src_ref=b_out.at[pl.ds(2 * k, 2)],
            dst_ref=b_in.at[it, k % 2 * NY + k // 2],
            send_sem=b_send.at[k],
            recv_sem=b_recv.at[it, k],
            device_id={"col": k},
            device_id_type=MESH,
        )

    def multiply(it, s, rel):
        block = block_of(rel)
        here = s % 4
        for chunk in range(LANES // 256):
            rows = slice(chunk * 256, (chunk + 1) * 256)
            prod[here, :, rows] = dot(t_pad[rows, : 2 * HALF], held[it, block]).T
        start = pl.multiple_of((1 - core) * 64, 64)
        mate_out[s] = prod[here, pl.ds(start, 64), :].astype(bf16)
        mate_copy(it, s).start()

    def add_mate(it, s):
        mate_copy(it, s).wait_recv()
        start = pl.multiple_of(core * 64, 64)
        sums[s] = (prod[s % 4, pl.ds(start, 64), :] + mate_in[it, s].astype(f32)).astype(bf16)
        for k in (2, 1, 3):
            y_copy(it, s, k).start()

    def add_y(it, s):
        total = sums[s, pl.ds(pl.multiple_of(y * PER, PER), PER)].astype(f32)
        for k in range(1, NY):
            y_copy(it, s, k).wait_recv()
            total += y_in[it, s, k - 1].astype(f32)
        if s == 0:
            s_in[it, row] = total.astype(bf16)
        else:
            z_out[s] = total.astype(bf16)
            z_copy(it, s).start()

    def prepare():
        for part in range(3):
            turned = contrast_ref[part].T * weight_ref[:, :NT]
            cw_ref[part] = jnp.concatenate([turned, jnp.zeros((NP, TPAD - NT), f32)], axis=1)
        lat[:, NQ * 32 :, :] = jnp.zeros((2, QPAD * 32 - NQ * 32, 128), f32)

    def pad_t():
        t_pad[656:, :] = jnp.zeros((LANES - 656, KPAD), bf16)
        t_pad[:, KPAD - 128 :] = jnp.zeros((LANES, 128), bf16)
        t_pad[:BLK, : 2 * BLK] = t_ref[...]

    def iteration(it, carry):
        s = 0
        for event in plan:
            if event[0] == "send":
                _, part, rel, way = event
                ring_copy(it, part, rel, way, slot[event[1:]]).start()
            elif event[0] == "recv":
                _, part, rel, way = event
                there = ((rel[0] + STEP[way][0]) % NX, (rel[1] + STEP[way][1]) % NZ)
                ring_copy(it, part, rel, way, slot[(part, there, way)]).wait_recv()
            else:
                if s == 0:
                    pl.when(it == 0)(pad_t)
                multiply(it, s, event[1])
                if s == 0:
                    pl.when(it == 0)(prepare)
                if s >= 3:
                    add_mate(it, s - 3)
                if s >= 7:
                    add_y(it, s - 7)
                s += 1
        add_mate(it, ROWS - 3)
        add_mate(it, ROWS - 2)
        add_y(it, ROWS - 7)
        add_mate(it, ROWS - 1)
        for late in range(ROWS - 6, ROWS):
            add_y(it, late)
        pl.when(it == 0)(table_copy.wait)
        for s in range(1, ROWS):
            z_arrival(it, s).wait_recv()

        def coefficients(block, window):
            lanes = slice(window * 128, (window + 1) * 128)
            return jnp.concatenate([s_in[it, block, :, lanes], s_in[it, block + 8, :, lanes]], axis=0)

        legendre_in(found, coefficients, w_ref, lat)
        columns(fs_ref, fa_ref, cw_ref, lat, spec)

        def done(k):
            @pl.when(col != k)
            def _():
                b_copy(it, k).start()

        legendre_out(found, w_ref, spec, b_out, done)
        b_in[it, core * NY + y] = b_out[pl.ds(2 * col, 2)]
        for event in plan:
            if event[0] == "send":
                _, part, rel, way = event
                ring_copy(it, part, rel, way, slot[event[1:]]).wait_send()
        for s in range(ROWS):
            mate_copy(it, s).wait_send()
            for k in range(1, NY):
                y_copy(it, s, k).wait_send()
            if s > 0:
                z_copy(it, s).wait_send()
        for k in range(COLS):

            @pl.when(col != k)
            def _():
                b_arrival(it, k).wait_recv()

        parts = []
        for half in range(2):
            value = jnp.concatenate([b_in[it, k, half].astype(f32) for k in range(COLS)], axis=0)
            parts.append(value.T[:BLK])
        value = (jnp.concatenate(parts, axis=0) + panel_ref[...].astype(f32)).astype(bf16)

        @pl.when(it == 0)
        def _():
            held[1, row, : 2 * BLK] = value

        @pl.when(it == 1)
        def _():
            out_ref[...] = value

        for k in range(COLS):

            @pl.when(col != k)
            def _():
                b_copy(it, k).wait_send()

        return carry

    lax.fori_loop(0, ITERS, iteration, 0)


def steps(t, panel, contrast, weight, w, fs, fa, found):
    plan = ring_plan()
    sends = sum(event[0] == "send" for event in plan)
    vmem = pl.BlockSpec(memory_space=pltpu.VMEM)
    dma = pltpu.SemaphoreType.DMA
    bf16, f32 = jnp.bfloat16, jnp.float32
    return pl.pallas_call(
        functools.partial(step_kernel, plan, found),
        out_shape=jax.ShapeDtypeStruct((2 * BLK, 128), bf16),
        in_specs=[vmem] * 4 + [pl.BlockSpec(memory_space=pl.ANY)] + [vmem] * 2,
        out_specs=vmem,
        scratch_shapes=[
            pltpu.VMEM((ITERS, ROWS, 2 * HALF, 128), bf16),
            pltpu.VMEM((4, 128, LANES), f32),
            pltpu.VMEM((ROWS, 64, LANES), bf16),
            pltpu.VMEM((ITERS, ROWS, 64, LANES), bf16),
            pltpu.VMEM((ROWS, 64, LANES), bf16),
            pltpu.VMEM((ITERS, ROWS, NY - 1, PER, LANES), bf16),
            pltpu.VMEM((ROWS, PER, LANES), bf16),
            pltpu.VMEM((ITERS, ROWS, PER, LANES), bf16),
            pltpu.VMEM((ROWS, PER, LANES), bf16),
            pltpu.VMEM((ITERS, COLS, 2, PER, LANES), bf16),
            pltpu.VMEM((LANES, KPAD), bf16),
            pltpu.VMEM(w.shape, bf16),
            pltpu.VMEM((3, NP, TPAD), f32),
            pltpu.VMEM((2, QPAD * 32, 128), f32),
            pltpu.VMEM((2, QPAD * 32, 128), f32),
            dma(()),
            dma((sends,)),
            dma((ITERS, sends)),
            dma((ROWS,)),
            dma((ITERS, ROWS)),
            dma((ROWS * 3,)),
            dma((ITERS, ROWS * 3)),
            dma((ROWS,)),
            dma((ITERS, ROWS)),
            dma((COLS,)),
            dma((ITERS, COLS)),
        ],
        compiler_params=pltpu.CompilerParams(
            collective_id=0, has_side_effects=True, vmem_limit_bytes=58 * MIB
        ),
        name="steps",
    )(t, panel, contrast, weight, w, fs, fa)


def body(tmatrix, panel, contrast):
    found, windows, fs, fa, weight = tables()
    weight = jnp.asarray(np.pad(weight, (0, TPAD - NT)).reshape(1, TPAD))
    return steps(
        tmatrix,
        panel,
        contrast,
        weight,
        jnp.asarray(windows),
        jnp.asarray(fs),
        jnp.asarray(fa),
        found,
    )


def solution(mesh):
    placed = (P("row", "col"), P("col", "row"), P())
    return jax.shard_map(
        body, mesh=mesh, in_specs=placed, out_specs=P("col", "row"), check_vma=False
    )
```

```python
import functools

import jax
import jax.numpy as jnp
import ml_dtypes
import numpy as np
from jax import lax
from jax.experimental import pallas as pl
from jax.experimental.pallas import tpu as pltpu
from jax.sharding import PartitionSpec as P

LDEG = 72
ITERS = 2
NT = 2 * LDEG
NP = 4 * LDEG
NQ = 2 * LDEG + 1
NX = 4
NZ = 4
NY = 4
ROWS = 16
COLS = 8
BLK = 666
HALF = 672
QUART = HALF // 2
LANES = 768
WIN = LANES // 128
TPAD = 256
KPAD = 1408
QPAD = 160
QH = QPAD // 2
PH = 160
PER = 16
MIB = 1024 * 1024
MESH = pl.DeviceIdType.MESH


def angular_tables(degree):
    lat_count = 2 * degree
    lon_count = 4 * degree
    freq_count = 2 * degree + 1
    colatitude = (np.arange(lat_count) + 0.5) * np.pi / lat_count
    cos_col = np.cos(colatitude)
    sin_col = np.sin(colatitude)
    legendre = np.zeros((freq_count, degree, lat_count))
    diagonal_term = np.full(lat_count, np.sqrt(0.5))
    for order_m in range(degree + 1):
        if order_m > 0:
            diagonal_term = (
                diagonal_term * np.sqrt((2.0 * order_m + 1.0) / (2.0 * order_m)) * sin_col
            )
        earlier = np.zeros(lat_count)
        latest = diagonal_term
        for degree_l in range(order_m, degree + 1):
            if degree_l == order_m:
                current = diagonal_term
            elif degree_l == order_m + 1:
                current = np.sqrt(2.0 * order_m + 3.0) * cos_col * diagonal_term
            else:
                factor_a = np.sqrt((4.0 * degree_l**2 - 1.0) / (degree_l**2 - order_m**2))
                factor_b = np.sqrt(
                    ((degree_l - 1.0) ** 2 - order_m**2) / (4.0 * (degree_l - 1.0) ** 2 - 1.0)
                )
                current = factor_a * (cos_col * latest - factor_b * earlier)
            if degree_l > order_m:
                earlier, latest = (latest, current)
            if degree_l >= 1:
                legendre[order_m, degree_l - 1] = current
                if order_m >= 1:
                    legendre[degree + order_m, degree_l - 1] = current
    longitude = 2.0 * np.pi * np.arange(lon_count) / lon_count
    fourier = np.zeros((freq_count, lon_count))
    fourier[0] = 1.0 / np.sqrt(2.0 * np.pi)
    for order_m in range(1, degree + 1):
        fourier[order_m] = np.cos(order_m * longitude) / np.sqrt(np.pi)
        fourier[degree + order_m] = np.sin(order_m * longitude) / np.sqrt(np.pi)
    weight = sin_col * (np.pi / lat_count) * (2.0 * np.pi / lon_count)
    return (legendre, fourier, weight)


def meetings():
    owner = []
    for q in range(NQ):
        m = q if q <= LDEG else q - LDEG
        owner += [(q, l) for l in range(max(m, 1), LDEG + 1)]
    found = []
    for block in range(ROWS // 2):
        for window in range(WIN):
            first = block * BLK + window * 128
            last = min(first + 128, (block + 1) * BLK)
            for q in sorted({owner[n][0] for n in range(first, last)}):
                rows = [(n - first, owner[n][1] - 1) for n in range(first, last) if owner[n][0] == q]
                found.append((block, window, q, rows))
    return found


def split(table):
    high = table.astype(np.float32).astype(ml_dtypes.bfloat16)
    low = (table - high.astype(np.float64)).astype(np.float32).astype(ml_dtypes.bfloat16)
    return np.stack([high, low])


@functools.lru_cache(None)
def tables():
    legendre, fourier, weight = angular_tables(LDEG)
    found = meetings()
    windows = np.zeros((len(found), 128, TPAD))
    for index, (block, window, q, rows) in enumerate(found):
        for place, level in rows:
            windows[index, place, :NT] = legendre[q, level]
    parts = np.zeros((2, QH, PH))
    parts[0, : LDEG + 1, : NP // 2 + 1] = fourier[: LDEG + 1, : NP // 2 + 1]
    parts[1, :LDEG, : NP // 2 + 1] = fourier[LDEG + 1 :, : NP // 2 + 1]
    high, low = split(parts)
    synthesis = np.concatenate([high, low, high], axis=1).transpose(0, 2, 1)
    analysis = np.concatenate([high, low], axis=1)
    mirror = np.zeros((2, PH, NP), np.float32)
    for p in range(NP // 2 + 1):
        mirror[0, p, p] = 1.0
        if 0 < p < NP // 2:
            mirror[1, p, NP - p] = 1.0
    return (
        [f[:3] for f in found],
        windows.astype(np.float32).astype(ml_dtypes.bfloat16),
        np.ascontiguousarray(synthesis),
        analysis,
        mirror.astype(ml_dtypes.bfloat16),
        weight.astype(np.float32),
    )


def dot(a, b):
    return jnp.dot(a, b, preferred_element_type=jnp.float32)


def two(value):
    high = value.astype(jnp.bfloat16)
    return high, (value - high.astype(jnp.float32)).astype(jnp.bfloat16)


def row_of(q):
    return 32 * (q if q <= LDEG else q - LDEG - 1 + QH)


def legendre_in(found, coefficients, w_ref, lat):
    by_q = {}
    for index, (block, window, q) in enumerate(found):
        by_q.setdefault(q, []).append((index, block, window))
    for q in range(NQ):
        total = None
        for index, block, window in by_q[q]:
            term = dot(coefficients(block, window), w_ref[index])
            total = term if total is None else total + term
        for half in range(2):
            lat[half, row_of(q) : row_of(q) + 32, :] = total[:, half * 128 : half * 128 + 128]


def columns(fs_ref, fa_ref, cw_ref, lat, spec):
    def synthesis(place):
        rows = pl.ds(place, QPAD, stride=32)
        high, low = two(jnp.concatenate([lat[0, rows, :], lat[1, rows, :]], axis=1))
        even, odd = [
            dot(fs_ref[k], jnp.concatenate([high[part], high[part], low[part]], axis=0))
            for k, part in enumerate((slice(0, QH), slice(QH, QPAD)))
        ]
        return even + odd, even - odd

    def analysis(place, values):
        found = []
        for k, value in enumerate((values[0] + values[1], values[0] - values[1])):
            high, low = two(value)
            both = dot(fa_ref[k], high)
            found.append(both[:QH] + both[QH:] + dot(fa_ref[k, :QH], low))
        value = jnp.concatenate(found, axis=0)
        for half in range(2):
            spec[half, pl.ds(place, QPAD, stride=32), :] = value[:, half * 128 : half * 128 + 128]

    def column(k, carry):
        first = synthesis(k)
        second = synthesis(PER + k)
        analysis(k, [cw_ref[i, 0] * first[i] + cw_ref[i, 1] * second[i] for i in range(2)])
        analysis(PER + k, [cw_ref[i, 1] * first[i] + cw_ref[i, 2] * second[i] for i in range(2)])
        return carry

    lax.fori_loop(0, PER, column, 0, unroll=4)


def legendre_out(found, w_ref, spec, b_ref, done):
    by_window = {}
    for index, (block, window, q) in enumerate(found):
        by_window.setdefault((block, window), []).append((index, q))
    for (block, window), members in sorted(by_window.items()):
        total = None
        for index, q in members:
            rows = slice(row_of(q), row_of(q) + 32)
            high, low = two(jnp.concatenate([spec[0, rows, :], spec[1, rows, :]], axis=1))
            term = lax.dot_general(
                jnp.concatenate([high, low], axis=0),
                w_ref[index],
                (((1,), (1,)), ((), ())),
                preferred_element_type=jnp.float32,
            )
            total = term if total is None else total + term
        value = (total[:32] + total[32:]).astype(jnp.bfloat16)
        lanes = slice(window * 128, (window + 1) * 128)
        b_ref[block, :, lanes] = value[:PER]
        b_ref[block + 8, :, lanes] = value[PER:]
        if window == WIN - 1 and block % 2 == 1:
            done(block // 2)
            done(block // 2 + 4)


STEP = {"x+": (1, 0), "x-": (-1, 0), "z+": (0, 1), "z-": (0, -1)}
ALL = (0, 2 * HALF)
A = (0, HALF)
B = (HALF, HALF)
A0, A1 = (0, QUART), (QUART, QUART)
B0, B1 = (HALF, QUART), (HALF + QUART, QUART)


def ring_plan():
    plan = []

    def send(part, rel, way):
        plan.append(("send", part, (rel[0] % NX, rel[1] % NZ), way))

    def recv(part, rel, way):
        plan.append(("recv", part, (rel[0] % NX, rel[1] % NZ), way))

    def use(*rels):
        for rel in rels:
            plan.append(("use", (rel[0] % NX, rel[1] % NZ)))

    own = (0, 0)
    for way in ("x+", "x-"):
        send(A, own, way)
    for way in ("z+", "z-"):
        send(B, own, way)
    for way in ("z+", "z-"):
        send(A, own, way)
    for way in ("x+", "x-"):
        send(B, own, way)
    use(own)
    for part, quart, rel, way in ((A, A0, (-1, 0), "x+"), (A, A1, (1, 0), "x-")):
        recv(part, rel, way)
        send(quart, rel, way)
        send(A, rel, "z+")
        send(A, rel, "z-")
    for part, quart, rel, way in ((B, B0, (0, -1), "z+"), (B, B1, (0, 1), "z-")):
        recv(part, rel, way)
        send(quart, rel, way)
        send(B, rel, "x+")
        send(B, rel, "x-")
    for quart, rel, way in ((A0, (0, -1), "z+"), (A1, (0, 1), "z-")):
        recv(A, rel, way)
        send(quart, rel, way)
    for quart, rel, way in ((B0, (-1, 0), "x+"), (B1, (1, 0), "x-")):
        recv(B, rel, way)
        send(quart, rel, way)
    use((-1, 0), (1, 0))
    recv(A0, (2, 0), "x+")
    recv(A1, (2, 0), "x-")
    send(A, (2, 0), "z+")
    send(A, (2, 0), "z-")
    recv(B0, (0, 2), "z+")
    recv(B1, (0, 2), "z-")
    send(B, (0, 2), "x+")
    send(B, (0, 2), "x-")
    use((0, -1), (0, 1))
    for x in (-1, 1):
        for quart, z, way in ((A0, -1, "z+"), (A1, 1, "z-")):
            recv(A, (x, z), way)
            send(quart, (x, z), way)
    for z in (-1, 1):
        for quart, x, way in ((B0, -1, "x+"), (B1, 1, "x-")):
            recv(B, (x, z), way)
            send(quart, (x, z), way)
    use((-1, -1), (-1, 1))
    recv(A0, (0, 2), "z+")
    recv(A1, (0, 2), "z-")
    recv(B0, (2, 0), "x+")
    recv(B1, (2, 0), "x-")
    for quart, z, way in ((A0, -1, "z+"), (A1, 1, "z-")):
        recv(A, (2, z), way)
        send(quart, (2, z), way)
    for quart, x, way in ((B0, -1, "x+"), (B1, 1, "x-")):
        recv(B, (x, 2), way)
        send(quart, (x, 2), way)
    use((1, -1), (1, 1), (0, 2), (2, 0))
    for x in (-1, 1):
        recv(A0, (x, 2), "z+")
        recv(A1, (x, 2), "z-")
        use((x, 2))
    for z in (-1, 1):
        recv(B0, (2, z), "x+")
        recv(B1, (2, z), "x-")
        use((2, z))
    recv(A0, (2, 2), "z+")
    recv(A1, (2, 2), "z-")
    recv(B0, (2, 2), "x+")
    recv(B1, (2, 2), "x-")
    use((2, 2))
    return plan


def greet(others):
    barrier = pltpu.get_barrier_semaphore()
    for other in others:
        pl.semaphore_signal(barrier, inc=1, device_id=other, device_id_type=MESH)
    pl.semaphore_wait(barrier, len(others))


def step_kernel(
    plan,
    found,
    t_ref,
    panel_ref,
    contrast_ref,
    weight_ref,
    w_hbm,
    fs_ref,
    fa_ref,
    mirror_ref,
    out_ref,
    held,
    prod,
    mate_out,
    mate_in,
    sums,
    y_in,
    z_out,
    s_in,
    b_out,
    b_in,
    t_pad,
    w_ref,
    cw_ref,
    lat,
    spec,
    w_sem,
    ring_send,
    ring_recv,
    mate_send,
    mate_recv,
    y_send,
    y_recv,
    z_send,
    z_recv,
    b_send,
    b_recv,
):
    row = lax.axis_index("row")
    col = lax.axis_index("col")
    x, z = row // NZ, row % NZ
    y, core = col // 2, col % 2
    f32, bf16 = jnp.float32, jnp.bfloat16

    def block_of(rel):
        return ((x + rel[0] + NX) % NX) * NZ + (z + rel[1] + NZ) % NZ

    table_copy = pltpu.make_async_copy(w_hbm, w_ref, w_sem)
    table_copy.start()
    for first in range(ITERS):
        held[first, row, 2 * HALF - 16 :] = jnp.zeros((16, 128), bf16)
    held[0, row, : 2 * BLK] = panel_ref[...]
    greet(
        [{"row": (row + k) % ROWS} for k in range(1, ROWS)]
        + [{"col": (col + k) % COLS} for k in range(1, COLS)]
    )
    mate = {"col": y * 2 + (1 - core)}
    y_peers = [{"col": ((y + k) % NY) * 2 + core} for k in range(1, NY)]

    slot = {}
    for event in plan:
        if event[0] == "send":
            slot[event[1:]] = len(slot)
    order = [event[1] for event in plan if event[0] == "use"]

    def ring_copy(it, part, rel, way, number):
        here = held.at[it, block_of(rel), pl.ds(part[0], part[1])]
        return pltpu.make_async_remote_copy(
            src_ref=here,
            dst_ref=here,
            send_sem=ring_send.at[number],
            recv_sem=ring_recv.at[it, number],
            device_id={"row": block_of(STEP[way])},
            device_id_type=MESH,
        )

    def mate_copy(it, s):
        return pltpu.make_async_remote_copy(
            src_ref=mate_out.at[s],
            dst_ref=mate_in.at[it, s],
            send_sem=mate_send.at[s],
            recv_sem=mate_recv.at[it, s],
            device_id=mate,
            device_id_type=MESH,
        )

    def y_copy(it, s, k):
        to = (y + k) % NY
        number = s * 3 + k - 1
        return pltpu.make_async_remote_copy(
            src_ref=sums.at[s, pl.ds(pl.multiple_of(to * PER, PER), PER)],
            dst_ref=y_in.at[it, s, k - 1],
            send_sem=y_send.at[number],
            recv_sem=y_recv.at[it, number],
            device_id=y_peers[k - 1],
            device_id_type=MESH,
        )

    def z_copy(it, s):
        return pltpu.make_async_remote_copy(
            src_ref=z_out.at[s],
            dst_ref=s_in.at[it, row],
            send_sem=z_send.at[s],
            recv_sem=z_recv.at[it, s],
            device_id={"row": block_of(order[s])},
            device_id_type=MESH,
        )

    def z_arrival(it, s):
        back = (-order[s][0], -order[s][1])
        return pltpu.make_async_remote_copy(
            src_ref=z_out.at[s],
            dst_ref=s_in.at[it, block_of(back)],
            send_sem=z_send.at[s],
            recv_sem=z_recv.at[it, s],
            device_id={"row": block_of(back)},
            device_id_type=MESH,
        )

    def b_copy(it, k):
        return pltpu.make_async_remote_copy(
            src_ref=b_out.at[pl.ds(2 * k, 2)],
            dst_ref=b_in.at[it, core * NY + y],
            send_sem=b_send.at[k],
            recv_sem=b_recv.at[it, col],
            device_id={"col": k},
            device_id_type=MESH,
        )

    def b_arrival(it, k):
        return pltpu.make_async_remote_copy(
            src_ref=b_out.at[pl.ds(2 * k, 2)],
            dst_ref=b_in.at[it, k % 2 * NY + k // 2],
            send_sem=b_send.at[k],
            recv_sem=b_recv.at[it, k],
            device_id={"col": k},
            device_id_type=MESH,
        )

    def multiply(it, s, rel):
        block = block_of(rel)
        here = s % 4
        for chunk in range(LANES // 256):
            rows = slice(chunk * 256, (chunk + 1) * 256)
            prod[here, :, rows] = dot(t_pad[rows, : 2 * HALF], held[it, block]).T
        start = pl.multiple_of((1 - core) * 64, 64)
        mate_out[s] = prod[here, pl.ds(start, 64), :].astype(bf16)
        mate_copy(it, s).start()

    def add_mate(it, s):
        mate_copy(it, s).wait_recv()
        start = pl.multiple_of(core * 64, 64)
        sums[s] = (prod[s % 4, pl.ds(start, 64), :] + mate_in[it, s].astype(f32)).astype(bf16)
        for k in (2, 1, 3):
            y_copy(it, s, k).start()

    def add_y(it, s):
        total = sums[s, pl.ds(pl.multiple_of(y * PER, PER), PER)].astype(f32)
        for k in range(1, NY):
            y_copy(it, s, k).wait_recv()
            total += y_in[it, s, k - 1].astype(f32)
        if s == 0:
            s_in[it, row] = total.astype(bf16)
        else:
            z_out[s] = total.astype(bf16)
            z_copy(it, s).start()

    def prepare():
        for part in range(3):
            turned = contrast_ref[part].T * weight_ref[:, :NT]
            turned = jnp.concatenate([turned, jnp.zeros((NP, TPAD - NT), f32)], axis=1)
            high, rest = turned.astype(bf16), turned
            pieces = []
            for _ in range(3):
                pieces.append(high)
                rest = rest - high.astype(f32)
                high = rest.astype(bf16)
            for side in range(2):
                picked = [dot(mirror_ref[side], piece) for piece in pieces]
                cw_ref[side, part] = picked[0] + picked[1] + picked[2]
        for first in (LDEG + 1, QH + LDEG):
            lat[:, first * 32 : (QH if first < QH else QPAD) * 32, :] = jnp.zeros(
                (2, ((QH if first < QH else QPAD) - first) * 32, 128), f32
            )

    def pad_t():
        t_pad[656:, :] = jnp.zeros((LANES - 656, KPAD), bf16)
        t_pad[:, KPAD - 128 :] = jnp.zeros((LANES, 128), bf16)
        t_pad[:BLK, : 2 * BLK] = t_ref[...]

    def iteration(it, carry):
        s = 0
        for event in plan:
            if event[0] == "send":
                _, part, rel, way = event
                ring_copy(it, part, rel, way, slot[event[1:]]).start()
            elif event[0] == "recv":
                _, part, rel, way = event
                there = ((rel[0] + STEP[way][0]) % NX, (rel[1] + STEP[way][1]) % NZ)
                ring_copy(it, part, rel, way, slot[(part, there, way)]).wait_recv()
            else:
                if s == 0:
                    pl.when(it == 0)(pad_t)
                multiply(it, s, event[1])
                if s == 0:
                    pl.when(it == 0)(prepare)
                if s >= 3:
                    add_mate(it, s - 3)
                if s >= 7:
                    add_y(it, s - 7)
                s += 1
        add_mate(it, ROWS - 3)
        add_mate(it, ROWS - 2)
        add_y(it, ROWS - 7)
        add_mate(it, ROWS - 1)
        for late in range(ROWS - 6, ROWS):
            add_y(it, late)
        pl.when(it == 0)(table_copy.wait)
        for s in range(1, ROWS):
            z_arrival(it, s).wait_recv()

        def coefficients(block, window):
            lanes = slice(window * 128, (window + 1) * 128)
            return jnp.concatenate([s_in[it, block, :, lanes], s_in[it, block + 8, :, lanes]], axis=0)

        legendre_in(found, coefficients, w_ref, lat)
        columns(fs_ref, fa_ref, cw_ref, lat, spec)

        def done(k):
            @pl.when(col != k)
            def _():
                b_copy(it, k).start()

        legendre_out(found, w_ref, spec, b_out, done)
        b_in[it, core * NY + y] = b_out[pl.ds(2 * col, 2)]
        for event in plan:
            if event[0] == "send":
                _, part, rel, way = event
                ring_copy(it, part, rel, way, slot[event[1:]]).wait_send()
        for s in range(ROWS):
            mate_copy(it, s).wait_send()
            for k in range(1, NY):
                y_copy(it, s, k).wait_send()
            if s > 0:
                z_copy(it, s).wait_send()
        for k in range(COLS):

            @pl.when(col != k)
            def _():
                b_arrival(it, k).wait_recv()

        parts = []
        for half in range(2):
            value = jnp.concatenate([b_in[it, k, half].astype(f32) for k in range(COLS)], axis=0)
            parts.append(value.T[:BLK])
        value = (jnp.concatenate(parts, axis=0) + panel_ref[...].astype(f32)).astype(bf16)

        @pl.when(it == 0)
        def _():
            held[1, row, : 2 * BLK] = value

        @pl.when(it == 1)
        def _():
            out_ref[...] = value

        for k in range(COLS):

            @pl.when(col != k)
            def _():
                b_copy(it, k).wait_send()

        return carry

    lax.fori_loop(0, ITERS, iteration, 0)


def steps(t, panel, contrast, weight, w, fs, fa, mirror, found):
    plan = ring_plan()
    sends = sum(event[0] == "send" for event in plan)
    vmem = pl.BlockSpec(memory_space=pltpu.VMEM)
    dma = pltpu.SemaphoreType.DMA
    bf16, f32 = jnp.bfloat16, jnp.float32
    return pl.pallas_call(
        functools.partial(step_kernel, plan, found),
        out_shape=jax.ShapeDtypeStruct((2 * BLK, 128), bf16),
        in_specs=[vmem] * 4 + [pl.BlockSpec(memory_space=pl.ANY)] + [vmem] * 3,
        out_specs=vmem,
        scratch_shapes=[
            pltpu.VMEM((ITERS, ROWS, 2 * HALF, 128), bf16),
            pltpu.VMEM((4, 128, LANES), f32),
            pltpu.VMEM((ROWS, 64, LANES), bf16),
            pltpu.VMEM((ITERS, ROWS, 64, LANES), bf16),
            pltpu.VMEM((ROWS, 64, LANES), bf16),
            pltpu.VMEM((ITERS, ROWS, NY - 1, PER, LANES), bf16),
            pltpu.VMEM((ROWS, PER, LANES), bf16),
            pltpu.VMEM((ITERS, ROWS, PER, LANES), bf16),
            pltpu.VMEM((ROWS, PER, LANES), bf16),
            pltpu.VMEM((ITERS, COLS, 2, PER, LANES), bf16),
            pltpu.VMEM((LANES, KPAD), bf16),
            pltpu.VMEM(w.shape, bf16),
            pltpu.VMEM((2, 3, PH, TPAD), f32),
            pltpu.VMEM((2, QPAD * 32, 128), f32),
            pltpu.VMEM((2, QPAD * 32, 128), f32),
            dma(()),
            dma((sends,)),
            dma((ITERS, sends)),
            dma((ROWS,)),
            dma((ITERS, ROWS)),
            dma((ROWS * 3,)),
            dma((ITERS, ROWS * 3)),
            dma((ROWS,)),
            dma((ITERS, ROWS)),
            dma((COLS,)),
            dma((ITERS, COLS)),
        ],
        compiler_params=pltpu.CompilerParams(
            collective_id=0, has_side_effects=True, vmem_limit_bytes=58 * MIB
        ),
        name="steps",
    )(t, panel, contrast, weight, w, fs, fa, mirror)


def body(tmatrix, panel, contrast):
    found, windows, fs, fa, mirror, weight = tables()
    weight = jnp.asarray(np.pad(weight, (0, TPAD - NT)).reshape(1, TPAD))
    return steps(
        tmatrix,
        panel,
        contrast,
        weight,
        jnp.asarray(windows),
        jnp.asarray(fs),
        jnp.asarray(fa),
        jnp.asarray(mirror),
        found,
    )


def solution(mesh):
    placed = (P("row", "col"), P("col", "row"), P())
    return jax.shard_map(
        body, mesh=mesh, in_specs=placed, out_specs=P("col", "row"), check_vma=False
    )
```

```python
import functools

import jax
import jax.numpy as jnp
import ml_dtypes
import numpy as np
from jax import lax
from jax.experimental import pallas as pl
from jax.experimental.pallas import tpu as pltpu
from jax.sharding import PartitionSpec as P

LDEG = 72
ITERS = 2
NT = 2 * LDEG
NP = 4 * LDEG
NQ = 2 * LDEG + 1
NX = 4
NZ = 4
NY = 4
ROWS = 16
COLS = 8
BLK = 666
HALF = 672
QUART = HALF // 2
LANES = 768
WIN = LANES // 128
TPAD = 256
KPAD = 1408
QPAD = 160
QH = QPAD // 2
CS = 40
PH = 160
PER = 16
MIB = 1024 * 1024
MESH = pl.DeviceIdType.MESH


def angular_tables(degree):
    lat_count = 2 * degree
    lon_count = 4 * degree
    freq_count = 2 * degree + 1
    colatitude = (np.arange(lat_count) + 0.5) * np.pi / lat_count
    cos_col = np.cos(colatitude)
    sin_col = np.sin(colatitude)
    legendre = np.zeros((freq_count, degree, lat_count))
    diagonal_term = np.full(lat_count, np.sqrt(0.5))
    for order_m in range(degree + 1):
        if order_m > 0:
            diagonal_term = (
                diagonal_term * np.sqrt((2.0 * order_m + 1.0) / (2.0 * order_m)) * sin_col
            )
        earlier = np.zeros(lat_count)
        latest = diagonal_term
        for degree_l in range(order_m, degree + 1):
            if degree_l == order_m:
                current = diagonal_term
            elif degree_l == order_m + 1:
                current = np.sqrt(2.0 * order_m + 3.0) * cos_col * diagonal_term
            else:
                factor_a = np.sqrt((4.0 * degree_l**2 - 1.0) / (degree_l**2 - order_m**2))
                factor_b = np.sqrt(
                    ((degree_l - 1.0) ** 2 - order_m**2) / (4.0 * (degree_l - 1.0) ** 2 - 1.0)
                )
                current = factor_a * (cos_col * latest - factor_b * earlier)
            if degree_l > order_m:
                earlier, latest = (latest, current)
            if degree_l >= 1:
                legendre[order_m, degree_l - 1] = current
                if order_m >= 1:
                    legendre[degree + order_m, degree_l - 1] = current
    longitude = 2.0 * np.pi * np.arange(lon_count) / lon_count
    fourier = np.zeros((freq_count, lon_count))
    fourier[0] = 1.0 / np.sqrt(2.0 * np.pi)
    for order_m in range(1, degree + 1):
        fourier[order_m] = np.cos(order_m * longitude) / np.sqrt(np.pi)
        fourier[degree + order_m] = np.sin(order_m * longitude) / np.sqrt(np.pi)
    weight = sin_col * (np.pi / lat_count) * (2.0 * np.pi / lon_count)
    return (legendre, fourier, weight)


def meetings():
    owner = []
    for q in range(NQ):
        m = q if q <= LDEG else q - LDEG
        owner += [(q, l) for l in range(max(m, 1), LDEG + 1)]
    found = []
    for block in range(ROWS // 2):
        for window in range(WIN):
            first = block * BLK + window * 128
            last = min(first + 128, (block + 1) * BLK)
            for q in sorted({owner[n][0] for n in range(first, last)}):
                rows = [(n - first, owner[n][1] - 1) for n in range(first, last) if owner[n][0] == q]
                found.append((block, window, q, rows))
    return found


def split(table):
    high = table.astype(np.float32).astype(ml_dtypes.bfloat16)
    low = (table - high.astype(np.float64)).astype(np.float32).astype(ml_dtypes.bfloat16)
    return np.stack([high, low])


@functools.lru_cache(None)
def tables():
    legendre, fourier, weight = angular_tables(LDEG)
    found = meetings()
    windows = np.zeros((len(found), 128, TPAD))
    for index, (block, window, q, rows) in enumerate(found):
        for place, level in rows:
            windows[index, place, :NT] = legendre[q, level]
    parts = np.zeros((2, QH, PH))
    parts[0, : LDEG + 1, : NP // 2 + 1] = fourier[: LDEG + 1, : NP // 2 + 1]
    parts[1, :LDEG, : NP // 2 + 1] = fourier[LDEG + 1 :, : NP // 2 + 1]
    high, low = split(parts)
    synthesis = np.concatenate([high, low, high], axis=1).transpose(0, 2, 1)
    analysis = np.concatenate([high, low], axis=1)
    mirror = np.zeros((2, PH, NP), np.float32)
    for p in range(NP // 2 + 1):
        mirror[0, p, p] = 1.0
        if 0 < p < NP // 2:
            mirror[1, p, NP - p] = 1.0
    return (
        [f[:3] for f in found],
        windows.astype(np.float32).astype(ml_dtypes.bfloat16),
        np.ascontiguousarray(synthesis),
        analysis,
        mirror.astype(ml_dtypes.bfloat16),
        weight.astype(np.float32),
    )


def dot(a, b):
    return jnp.dot(a, b, preferred_element_type=jnp.float32)


def two(value):
    high = value.astype(jnp.bfloat16)
    return high, (value - high.astype(jnp.float32)).astype(jnp.bfloat16)


def row_of(q):
    return CS * (q if q <= LDEG else q - LDEG - 1 + QH)


def legendre_in(found, coefficients, w_ref, lat):
    by_q = {}
    for index, (block, window, q) in enumerate(found):
        by_q.setdefault(q, []).append((index, block, window))
    for q in range(NQ):
        total = None
        for index, block, window in by_q[q]:
            term = dot(coefficients(block, window), w_ref[index])
            total = term if total is None else total + term
        for half in range(2):
            lat[half, row_of(q) : row_of(q) + 32, :] = total[:, half * 128 : half * 128 + 128]


def columns(fs_ref, fa_ref, cw_ref, lat, spec):
    def synthesis(place):
        rows = pl.ds(place, QPAD, stride=CS)
        high, low = two(jnp.concatenate([lat[0, rows, :], lat[1, rows, :]], axis=1))
        even, odd = [
            dot(fs_ref[k], jnp.concatenate([high[part], high[part], low[part]], axis=0))
            for k, part in enumerate((slice(0, QH), slice(QH, QPAD)))
        ]
        return even + odd, even - odd

    def analysis(place, values):
        found = []
        for k, value in enumerate((values[0] + values[1], values[0] - values[1])):
            high, low = two(value)
            both = dot(fa_ref[k], high)
            found.append(both[:QH] + both[QH:] + dot(fa_ref[k, :QH], low))
        value = jnp.concatenate(found, axis=0)
        for half in range(2):
            spec[half, pl.ds(place, QPAD, stride=CS), :] = value[:, half * 128 : half * 128 + 128]

    def column(k, carry):
        first = synthesis(k)
        second = synthesis(PER + k)
        analysis(k, [cw_ref[i, 0] * first[i] + cw_ref[i, 1] * second[i] for i in range(2)])
        analysis(PER + k, [cw_ref[i, 1] * first[i] + cw_ref[i, 2] * second[i] for i in range(2)])
        return carry

    lax.fori_loop(0, PER, column, 0, unroll=4)


def legendre_out(found, w_ref, spec, b_ref, done):
    by_window = {}
    for index, (block, window, q) in enumerate(found):
        by_window.setdefault((block, window), []).append((index, q))
    for (block, window), members in sorted(by_window.items()):
        total = None
        for index, q in members:
            rows = slice(row_of(q), row_of(q) + 32)
            high, low = two(jnp.concatenate([spec[0, rows, :], spec[1, rows, :]], axis=1))
            term = lax.dot_general(
                jnp.concatenate([high, low], axis=0),
                w_ref[index],
                (((1,), (1,)), ((), ())),
                preferred_element_type=jnp.float32,
            )
            total = term if total is None else total + term
        value = (total[:32] + total[32:]).astype(jnp.bfloat16)
        lanes = slice(window * 128, (window + 1) * 128)
        b_ref[block, :, lanes] = value[:PER]
        b_ref[block + 8, :, lanes] = value[PER:]
        if window == WIN - 1 and block % 2 == 1:
            done(block // 2)
            done(block // 2 + 4)


STEP = {"x+": (1, 0), "x-": (-1, 0), "z+": (0, 1), "z-": (0, -1)}
ALL = (0, 2 * HALF)
A = (0, HALF)
B = (HALF, HALF)
A0, A1 = (0, QUART), (QUART, QUART)
B0, B1 = (HALF, QUART), (HALF + QUART, QUART)


def ring_plan():
    plan = []

    def send(part, rel, way):
        plan.append(("send", part, (rel[0] % NX, rel[1] % NZ), way))

    def recv(part, rel, way):
        plan.append(("recv", part, (rel[0] % NX, rel[1] % NZ), way))

    def use(*rels):
        for rel in rels:
            plan.append(("use", (rel[0] % NX, rel[1] % NZ)))

    own = (0, 0)
    for way in ("x+", "x-"):
        send(A, own, way)
    for way in ("z+", "z-"):
        send(B, own, way)
    for way in ("z+", "z-"):
        send(A, own, way)
    for way in ("x+", "x-"):
        send(B, own, way)
    use(own)
    for part, quart, rel, way in ((A, A0, (-1, 0), "x+"), (A, A1, (1, 0), "x-")):
        recv(part, rel, way)
        send(quart, rel, way)
        send(A, rel, "z+")
        send(A, rel, "z-")
    for part, quart, rel, way in ((B, B0, (0, -1), "z+"), (B, B1, (0, 1), "z-")):
        recv(part, rel, way)
        send(quart, rel, way)
        send(B, rel, "x+")
        send(B, rel, "x-")
    for quart, rel, way in ((A0, (0, -1), "z+"), (A1, (0, 1), "z-")):
        recv(A, rel, way)
        send(quart, rel, way)
    for quart, rel, way in ((B0, (-1, 0), "x+"), (B1, (1, 0), "x-")):
        recv(B, rel, way)
        send(quart, rel, way)
    use((-1, 0), (1, 0))
    recv(A0, (2, 0), "x+")
    recv(A1, (2, 0), "x-")
    send(A, (2, 0), "z+")
    send(A, (2, 0), "z-")
    recv(B0, (0, 2), "z+")
    recv(B1, (0, 2), "z-")
    send(B, (0, 2), "x+")
    send(B, (0, 2), "x-")
    use((0, -1), (0, 1))
    for x in (-1, 1):
        for quart, z, way in ((A0, -1, "z+"), (A1, 1, "z-")):
            recv(A, (x, z), way)
            send(quart, (x, z), way)
    for z in (-1, 1):
        for quart, x, way in ((B0, -1, "x+"), (B1, 1, "x-")):
            recv(B, (x, z), way)
            send(quart, (x, z), way)
    use((-1, -1), (-1, 1))
    recv(A0, (0, 2), "z+")
    recv(A1, (0, 2), "z-")
    recv(B0, (2, 0), "x+")
    recv(B1, (2, 0), "x-")
    for quart, z, way in ((A0, -1, "z+"), (A1, 1, "z-")):
        recv(A, (2, z), way)
        send(quart, (2, z), way)
    for quart, x, way in ((B0, -1, "x+"), (B1, 1, "x-")):
        recv(B, (x, 2), way)
        send(quart, (x, 2), way)
    use((1, -1), (1, 1), (0, 2), (2, 0))
    for x in (-1, 1):
        recv(A0, (x, 2), "z+")
        recv(A1, (x, 2), "z-")
        use((x, 2))
    for z in (-1, 1):
        recv(B0, (2, z), "x+")
        recv(B1, (2, z), "x-")
        use((2, z))
    recv(A0, (2, 2), "z+")
    recv(A1, (2, 2), "z-")
    recv(B0, (2, 2), "x+")
    recv(B1, (2, 2), "x-")
    use((2, 2))
    return plan


def greet(others):
    barrier = pltpu.get_barrier_semaphore()
    for other in others:
        pl.semaphore_signal(barrier, inc=1, device_id=other, device_id_type=MESH)
    pl.semaphore_wait(barrier, len(others))


def step_kernel(
    plan,
    found,
    t_ref,
    panel_ref,
    contrast_ref,
    weight_ref,
    w_hbm,
    fs_ref,
    fa_ref,
    mirror_ref,
    out_ref,
    held,
    prod,
    mate_out,
    mate_in,
    sums,
    y_in,
    z_out,
    s_in,
    b_out,
    b_in,
    t_pad,
    w_ref,
    cw_ref,
    lat,
    spec,
    w_sem,
    ring_send,
    ring_recv,
    mate_send,
    mate_recv,
    y_send,
    y_recv,
    z_send,
    z_recv,
    b_send,
    b_recv,
):
    row = lax.axis_index("row")
    col = lax.axis_index("col")
    x, z = row // NZ, row % NZ
    y, core = col // 2, col % 2
    f32, bf16 = jnp.float32, jnp.bfloat16

    def block_of(rel):
        return ((x + rel[0] + NX) % NX) * NZ + (z + rel[1] + NZ) % NZ

    table_copy = pltpu.make_async_copy(w_hbm, w_ref, w_sem)
    table_copy.start()
    for first in range(ITERS):
        held[first, row, 2 * HALF - 16 :] = jnp.zeros((16, 128), bf16)
    held[0, row, : 2 * BLK] = panel_ref[...]
    greet(
        [{"row": (row + k) % ROWS} for k in range(1, ROWS)]
        + [{"col": (col + k) % COLS} for k in range(1, COLS)]
    )
    mate = {"col": y * 2 + (1 - core)}
    y_peers = [{"col": ((y + k) % NY) * 2 + core} for k in range(1, NY)]

    slot = {}
    for event in plan:
        if event[0] == "send":
            slot[event[1:]] = len(slot)
    order = [event[1] for event in plan if event[0] == "use"]

    def ring_copy(it, part, rel, way, number):
        here = held.at[it, block_of(rel), pl.ds(part[0], part[1])]
        return pltpu.make_async_remote_copy(
            src_ref=here,
            dst_ref=here,
            send_sem=ring_send.at[number],
            recv_sem=ring_recv.at[it, number],
            device_id={"row": block_of(STEP[way])},
            device_id_type=MESH,
        )

    def mate_copy(it, s):
        return pltpu.make_async_remote_copy(
            src_ref=mate_out.at[s],
            dst_ref=mate_in.at[it, s],
            send_sem=mate_send.at[s],
            recv_sem=mate_recv.at[it, s],
            device_id=mate,
            device_id_type=MESH,
        )

    def y_copy(it, s, k):
        to = (y + k) % NY
        number = s * 3 + k - 1
        return pltpu.make_async_remote_copy(
            src_ref=sums.at[s, pl.ds(pl.multiple_of(to * PER, PER), PER)],
            dst_ref=y_in.at[it, s, k - 1],
            send_sem=y_send.at[number],
            recv_sem=y_recv.at[it, number],
            device_id=y_peers[k - 1],
            device_id_type=MESH,
        )

    def z_copy(it, s):
        return pltpu.make_async_remote_copy(
            src_ref=z_out.at[s],
            dst_ref=s_in.at[it, row],
            send_sem=z_send.at[s],
            recv_sem=z_recv.at[it, s],
            device_id={"row": block_of(order[s])},
            device_id_type=MESH,
        )

    def z_arrival(it, s):
        back = (-order[s][0], -order[s][1])
        return pltpu.make_async_remote_copy(
            src_ref=z_out.at[s],
            dst_ref=s_in.at[it, block_of(back)],
            send_sem=z_send.at[s],
            recv_sem=z_recv.at[it, s],
            device_id={"row": block_of(back)},
            device_id_type=MESH,
        )

    def b_copy(it, k):
        return pltpu.make_async_remote_copy(
            src_ref=b_out.at[pl.ds(2 * k, 2)],
            dst_ref=b_in.at[it, core * NY + y],
            send_sem=b_send.at[k],
            recv_sem=b_recv.at[it, col],
            device_id={"col": k},
            device_id_type=MESH,
        )

    def b_arrival(it, k):
        return pltpu.make_async_remote_copy(
            src_ref=b_out.at[pl.ds(2 * k, 2)],
            dst_ref=b_in.at[it, k % 2 * NY + k // 2],
            send_sem=b_send.at[k],
            recv_sem=b_recv.at[it, k],
            device_id={"col": k},
            device_id_type=MESH,
        )

    def multiply(it, s, rel):
        block = block_of(rel)
        here = s % 4
        for chunk in range(LANES // 256):
            rows = slice(chunk * 256, (chunk + 1) * 256)
            prod[here, :, rows] = dot(t_pad[rows, : 2 * HALF], held[it, block]).T
        start = pl.multiple_of((1 - core) * 64, 64)
        mate_out[s] = prod[here, pl.ds(start, 64), :].astype(bf16)
        mate_copy(it, s).start()

    def add_mate(it, s):
        mate_copy(it, s).wait_recv()
        start = pl.multiple_of(core * 64, 64)
        sums[s] = (prod[s % 4, pl.ds(start, 64), :] + mate_in[it, s].astype(f32)).astype(bf16)
        for k in (2, 1, 3):
            y_copy(it, s, k).start()

    def add_y(it, s):
        total = sums[s, pl.ds(pl.multiple_of(y * PER, PER), PER)].astype(f32)
        for k in range(1, NY):
            y_copy(it, s, k).wait_recv()
            total += y_in[it, s, k - 1].astype(f32)
        if s == 0:
            s_in[it, row] = total.astype(bf16)
        else:
            z_out[s] = total.astype(bf16)
            z_copy(it, s).start()

    def prepare():
        for part in range(3):
            turned = contrast_ref[part].T * weight_ref[:, :NT]
            turned = jnp.concatenate([turned, jnp.zeros((NP, TPAD - NT), f32)], axis=1)
            high, rest = turned.astype(bf16), turned
            pieces = []
            for _ in range(3):
                pieces.append(high)
                rest = rest - high.astype(f32)
                high = rest.astype(bf16)
            for side in range(2):
                picked = [dot(mirror_ref[side], piece) for piece in pieces]
                cw_ref[side, part] = picked[0] + picked[1] + picked[2]
        for first in (LDEG + 1, QH + LDEG):
            lat[:, first * CS : (QH if first < QH else QPAD) * CS, :] = jnp.zeros(
                (2, ((QH if first < QH else QPAD) - first) * CS, 128), f32
            )

    def pad_t():
        t_pad[656:, :] = jnp.zeros((LANES - 656, KPAD), bf16)
        t_pad[:, KPAD - 128 :] = jnp.zeros((LANES, 128), bf16)
        t_pad[:BLK, : 2 * BLK] = t_ref[...]

    def iteration(it, carry):
        s = 0
        for event in plan:
            if event[0] == "send":
                _, part, rel, way = event
                ring_copy(it, part, rel, way, slot[event[1:]]).start()
            elif event[0] == "recv":
                _, part, rel, way = event
                there = ((rel[0] + STEP[way][0]) % NX, (rel[1] + STEP[way][1]) % NZ)
                ring_copy(it, part, rel, way, slot[(part, there, way)]).wait_recv()
            else:
                if s == 0:
                    pl.when(it == 0)(pad_t)
                multiply(it, s, event[1])
                if s == 0:
                    pl.when(it == 0)(prepare)
                if s >= 3:
                    add_mate(it, s - 3)
                if s >= 7:
                    add_y(it, s - 7)
                s += 1
        add_mate(it, ROWS - 3)
        add_mate(it, ROWS - 2)
        add_y(it, ROWS - 7)
        add_mate(it, ROWS - 1)
        for late in range(ROWS - 6, ROWS):
            add_y(it, late)
        pl.when(it == 0)(table_copy.wait)
        for s in range(1, ROWS):
            z_arrival(it, s).wait_recv()

        def coefficients(block, window):
            lanes = slice(window * 128, (window + 1) * 128)
            return jnp.concatenate([s_in[it, block, :, lanes], s_in[it, block + 8, :, lanes]], axis=0)

        legendre_in(found, coefficients, w_ref, lat)
        columns(fs_ref, fa_ref, cw_ref, lat, spec)

        def done(k):
            @pl.when(col != k)
            def _():
                b_copy(it, k).start()

        legendre_out(found, w_ref, spec, b_out, done)
        b_in[it, core * NY + y] = b_out[pl.ds(2 * col, 2)]
        for event in plan:
            if event[0] == "send":
                _, part, rel, way = event
                ring_copy(it, part, rel, way, slot[event[1:]]).wait_send()
        for s in range(ROWS):
            mate_copy(it, s).wait_send()
            for k in range(1, NY):
                y_copy(it, s, k).wait_send()
            if s > 0:
                z_copy(it, s).wait_send()
        for k in range(COLS):

            @pl.when(col != k)
            def _():
                b_arrival(it, k).wait_recv()

        parts = []
        for half in range(2):
            value = jnp.concatenate([b_in[it, k, half].astype(f32) for k in range(COLS)], axis=0)
            parts.append(value.T[:BLK])
        value = (jnp.concatenate(parts, axis=0) + panel_ref[...].astype(f32)).astype(bf16)

        @pl.when(it == 0)
        def _():
            held[1, row, : 2 * BLK] = value

        @pl.when(it == 1)
        def _():
            out_ref[...] = value

        for k in range(COLS):

            @pl.when(col != k)
            def _():
                b_copy(it, k).wait_send()

        return carry

    lax.fori_loop(0, ITERS, iteration, 0)


def steps(t, panel, contrast, weight, w, fs, fa, mirror, found):
    plan = ring_plan()
    sends = sum(event[0] == "send" for event in plan)
    vmem = pl.BlockSpec(memory_space=pltpu.VMEM)
    dma = pltpu.SemaphoreType.DMA
    bf16, f32 = jnp.bfloat16, jnp.float32
    return pl.pallas_call(
        functools.partial(step_kernel, plan, found),
        out_shape=jax.ShapeDtypeStruct((2 * BLK, 128), bf16),
        in_specs=[vmem] * 4 + [pl.BlockSpec(memory_space=pl.ANY)] + [vmem] * 3,
        out_specs=vmem,
        scratch_shapes=[
            pltpu.VMEM((ITERS, ROWS, 2 * HALF, 128), bf16),
            pltpu.VMEM((4, 128, LANES), f32),
            pltpu.VMEM((ROWS, 64, LANES), bf16),
            pltpu.VMEM((ITERS, ROWS, 64, LANES), bf16),
            pltpu.VMEM((ROWS, 64, LANES), bf16),
            pltpu.VMEM((ITERS, ROWS, NY - 1, PER, LANES), bf16),
            pltpu.VMEM((ROWS, PER, LANES), bf16),
            pltpu.VMEM((ITERS, ROWS, PER, LANES), bf16),
            pltpu.VMEM((ROWS, PER, LANES), bf16),
            pltpu.VMEM((ITERS, COLS, 2, PER, LANES), bf16),
            pltpu.VMEM((LANES, KPAD), bf16),
            pltpu.VMEM(w.shape, bf16),
            pltpu.VMEM((2, 3, PH, TPAD), f32),
            pltpu.VMEM((2, QPAD * CS, 128), f32),
            pltpu.VMEM((2, QPAD * CS, 128), f32),
            dma(()),
            dma((sends,)),
            dma((ITERS, sends)),
            dma((ROWS,)),
            dma((ITERS, ROWS)),
            dma((ROWS * 3,)),
            dma((ITERS, ROWS * 3)),
            dma((ROWS,)),
            dma((ITERS, ROWS)),
            dma((COLS,)),
            dma((ITERS, COLS)),
        ],
        compiler_params=pltpu.CompilerParams(
            collective_id=0, has_side_effects=True, vmem_limit_bytes=58 * MIB
        ),
        name="steps",
    )(t, panel, contrast, weight, w, fs, fa, mirror)


def body(tmatrix, panel, contrast):
    found, windows, fs, fa, mirror, weight = tables()
    weight = jnp.asarray(np.pad(weight, (0, TPAD - NT)).reshape(1, TPAD))
    return steps(
        tmatrix,
        panel,
        contrast,
        weight,
        jnp.asarray(windows),
        jnp.asarray(fs),
        jnp.asarray(fa),
        jnp.asarray(mirror),
        found,
    )


def solution(mesh):
    placed = (P("row", "col"), P("col", "row"), P())
    return jax.shard_map(
        body, mesh=mesh, in_specs=placed, out_specs=P("col", "row"), check_vma=False
    )
```

```python
import functools

import jax
import jax.numpy as jnp
import ml_dtypes
import numpy as np
from jax import lax
from jax.experimental import pallas as pl
from jax.experimental.pallas import tpu as pltpu
from jax.sharding import PartitionSpec as P

LDEG = 72
ITERS = 2
NT = 2 * LDEG
NP = 4 * LDEG
NQ = 2 * LDEG + 1
NX = 4
NZ = 4
NY = 4
ROWS = 16
COLS = 8
BLK = 666
HALF = 672
QUART = HALF // 2
LANES = 768
WIN = LANES // 128
TPAD = 256
KPAD = 1408
QPAD = 160
QH = QPAD // 2
CS = 40
PH = 160
PER = 16
MIB = 1024 * 1024
MESH = pl.DeviceIdType.MESH


def angular_tables(degree):
    lat_count = 2 * degree
    lon_count = 4 * degree
    freq_count = 2 * degree + 1
    colatitude = (np.arange(lat_count) + 0.5) * np.pi / lat_count
    cos_col = np.cos(colatitude)
    sin_col = np.sin(colatitude)
    legendre = np.zeros((freq_count, degree, lat_count))
    diagonal_term = np.full(lat_count, np.sqrt(0.5))
    for order_m in range(degree + 1):
        if order_m > 0:
            diagonal_term = (
                diagonal_term * np.sqrt((2.0 * order_m + 1.0) / (2.0 * order_m)) * sin_col
            )
        earlier = np.zeros(lat_count)
        latest = diagonal_term
        for degree_l in range(order_m, degree + 1):
            if degree_l == order_m:
                current = diagonal_term
            elif degree_l == order_m + 1:
                current = np.sqrt(2.0 * order_m + 3.0) * cos_col * diagonal_term
            else:
                factor_a = np.sqrt((4.0 * degree_l**2 - 1.0) / (degree_l**2 - order_m**2))
                factor_b = np.sqrt(
                    ((degree_l - 1.0) ** 2 - order_m**2) / (4.0 * (degree_l - 1.0) ** 2 - 1.0)
                )
                current = factor_a * (cos_col * latest - factor_b * earlier)
            if degree_l > order_m:
                earlier, latest = (latest, current)
            if degree_l >= 1:
                legendre[order_m, degree_l - 1] = current
                if order_m >= 1:
                    legendre[degree + order_m, degree_l - 1] = current
    longitude = 2.0 * np.pi * np.arange(lon_count) / lon_count
    fourier = np.zeros((freq_count, lon_count))
    fourier[0] = 1.0 / np.sqrt(2.0 * np.pi)
    for order_m in range(1, degree + 1):
        fourier[order_m] = np.cos(order_m * longitude) / np.sqrt(np.pi)
        fourier[degree + order_m] = np.sin(order_m * longitude) / np.sqrt(np.pi)
    weight = sin_col * (np.pi / lat_count) * (2.0 * np.pi / lon_count)
    return (legendre, fourier, weight)


def meetings():
    owner = []
    for q in range(NQ):
        m = q if q <= LDEG else q - LDEG
        owner += [(q, l) for l in range(max(m, 1), LDEG + 1)]
    found = []
    for block in range(ROWS // 2):
        for window in range(WIN):
            first = block * BLK + window * 128
            last = min(first + 128, (block + 1) * BLK)
            for q in sorted({owner[n][0] for n in range(first, last)}):
                rows = [(n - first, owner[n][1] - 1) for n in range(first, last) if owner[n][0] == q]
                found.append((block, window, q, rows))
    return found


def split(table):
    high = table.astype(np.float32).astype(ml_dtypes.bfloat16)
    low = (table - high.astype(np.float64)).astype(np.float32).astype(ml_dtypes.bfloat16)
    return np.stack([high, low])


@functools.lru_cache(None)
def tables():
    legendre, fourier, weight = angular_tables(LDEG)
    found = meetings()
    windows = np.zeros((len(found), 128, TPAD))
    for index, (block, window, q, rows) in enumerate(found):
        for place, level in rows:
            windows[index, place, :NT] = legendre[q, level]
    parts = np.zeros((2, QH, PH))
    parts[0, : LDEG + 1, : NP // 2 + 1] = fourier[: LDEG + 1, : NP // 2 + 1]
    parts[1, :LDEG, : NP // 2 + 1] = fourier[LDEG + 1 :, : NP // 2 + 1]
    high, low = split(parts)
    synthesis = np.concatenate([high, low, high], axis=1).transpose(0, 2, 1)
    analysis = np.concatenate([high, low], axis=1)
    mirror = np.zeros((2, PH, NP), np.float32)
    for p in range(NP // 2 + 1):
        mirror[0, p, p] = 1.0
        if 0 < p < NP // 2:
            mirror[1, p, NP - p] = 1.0
    return (
        [f[:3] for f in found],
        windows.astype(np.float32).astype(ml_dtypes.bfloat16),
        np.ascontiguousarray(synthesis),
        analysis,
        mirror.astype(ml_dtypes.bfloat16),
        weight.astype(np.float32),
    )


def dot(a, b):
    return jnp.dot(a, b, preferred_element_type=jnp.float32)


def two(value):
    high = value.astype(jnp.bfloat16)
    return high, (value - high.astype(jnp.float32)).astype(jnp.bfloat16)


def row_of(q):
    return CS * (q if q <= LDEG else q - LDEG - 1 + QH)


def legendre_in(found, coefficients, w_ref, lat):
    by_q = {}
    for index, (block, window, q) in enumerate(found):
        by_q.setdefault(q, []).append((index, block, window))
    for q in range(NQ):
        total = None
        for index, block, window in by_q[q]:
            term = dot(coefficients(block, window), w_ref[index])
            total = term if total is None else total + term
        for half in range(2):
            lat[half, row_of(q) : row_of(q) + 32, :] = total[:, half * 128 : half * 128 + 128]


def columns(fs_ref, fa_ref, cw_ref, lat, spec):
    def synthesis(place):
        rows = pl.ds(place, QPAD, stride=CS)
        high, low = two(jnp.concatenate([lat[0, rows, :], lat[1, rows, :]], axis=1))
        even, odd = [
            dot(fs_ref[k], jnp.concatenate([high[part], high[part], low[part]], axis=0))
            for k, part in enumerate((slice(0, QH), slice(QH, QPAD)))
        ]
        return even + odd, even - odd

    def analysis(place, values):
        found = []
        for k, value in enumerate((values[0] + values[1], values[0] - values[1])):
            high, low = two(value)
            both = dot(fa_ref[k], high)
            found.append(both[:QH] + both[QH:] + dot(fa_ref[k, :QH], low))
        value = jnp.concatenate(found, axis=0)
        for half in range(2):
            spec[half, pl.ds(place, QPAD, stride=CS), :] = value[:, half * 128 : half * 128 + 128]

    def column(k, carry):
        first = synthesis(k)
        second = synthesis(PER + k)
        analysis(k, [cw_ref[i, 0] * first[i] + cw_ref[i, 1] * second[i] for i in range(2)])
        analysis(PER + k, [cw_ref[i, 1] * first[i] + cw_ref[i, 2] * second[i] for i in range(2)])
        return carry

    lax.fori_loop(0, PER, column, 0, unroll=8)


def legendre_out(found, w_ref, spec, b_ref, done):
    by_window = {}
    for index, (block, window, q) in enumerate(found):
        by_window.setdefault((block, window), []).append((index, q))
    for (block, window), members in sorted(by_window.items()):
        total = None
        for index, q in members:
            rows = slice(row_of(q), row_of(q) + 32)
            high, low = two(jnp.concatenate([spec[0, rows, :], spec[1, rows, :]], axis=1))
            term = lax.dot_general(
                jnp.concatenate([high, low], axis=0),
                w_ref[index],
                (((1,), (1,)), ((), ())),
                preferred_element_type=jnp.float32,
            )
            total = term if total is None else total + term
        value = (total[:32] + total[32:]).astype(jnp.bfloat16)
        lanes = slice(window * 128, (window + 1) * 128)
        b_ref[block, :, lanes] = value[:PER]
        b_ref[block + 8, :, lanes] = value[PER:]
        if window == WIN - 1 and block % 2 == 1:
            done(block // 2)
            done(block // 2 + 4)


STEP = {"x+": (1, 0), "x-": (-1, 0), "z+": (0, 1), "z-": (0, -1)}
ALL = (0, 2 * HALF)
A = (0, HALF)
B = (HALF, HALF)
A0, A1 = (0, QUART), (QUART, QUART)
B0, B1 = (HALF, QUART), (HALF + QUART, QUART)


def ring_plan():
    plan = []

    def send(part, rel, way):
        plan.append(("send", part, (rel[0] % NX, rel[1] % NZ), way))

    def recv(part, rel, way):
        plan.append(("recv", part, (rel[0] % NX, rel[1] % NZ), way))

    def use(*rels):
        for rel in rels:
            plan.append(("use", (rel[0] % NX, rel[1] % NZ)))

    own = (0, 0)
    for way in ("x+", "x-"):
        send(A, own, way)
    for way in ("z+", "z-"):
        send(B, own, way)
    for way in ("z+", "z-"):
        send(A, own, way)
    for way in ("x+", "x-"):
        send(B, own, way)
    use(own)
    for part, quart, rel, way in ((A, A0, (-1, 0), "x+"), (A, A1, (1, 0), "x-")):
        recv(part, rel, way)
        send(quart, rel, way)
        send(A, rel, "z+")
        send(A, rel, "z-")
    for part, quart, rel, way in ((B, B0, (0, -1), "z+"), (B, B1, (0, 1), "z-")):
        recv(part, rel, way)
        send(quart, rel, way)
        send(B, rel, "x+")
        send(B, rel, "x-")
    for quart, rel, way in ((A0, (0, -1), "z+"), (A1, (0, 1), "z-")):
        recv(A, rel, way)
        send(quart, rel, way)
    for quart, rel, way in ((B0, (-1, 0), "x+"), (B1, (1, 0), "x-")):
        recv(B, rel, way)
        send(quart, rel, way)
    use((-1, 0), (1, 0))
    recv(A0, (2, 0), "x+")
    recv(A1, (2, 0), "x-")
    send(A, (2, 0), "z+")
    send(A, (2, 0), "z-")
    recv(B0, (0, 2), "z+")
    recv(B1, (0, 2), "z-")
    send(B, (0, 2), "x+")
    send(B, (0, 2), "x-")
    use((0, -1), (0, 1))
    for x in (-1, 1):
        for quart, z, way in ((A0, -1, "z+"), (A1, 1, "z-")):
            recv(A, (x, z), way)
            send(quart, (x, z), way)
    for z in (-1, 1):
        for quart, x, way in ((B0, -1, "x+"), (B1, 1, "x-")):
            recv(B, (x, z), way)
            send(quart, (x, z), way)
    use((-1, -1), (-1, 1))
    recv(A0, (0, 2), "z+")
    recv(A1, (0, 2), "z-")
    recv(B0, (2, 0), "x+")
    recv(B1, (2, 0), "x-")
    for quart, z, way in ((A0, -1, "z+"), (A1, 1, "z-")):
        recv(A, (2, z), way)
        send(quart, (2, z), way)
    for quart, x, way in ((B0, -1, "x+"), (B1, 1, "x-")):
        recv(B, (x, 2), way)
        send(quart, (x, 2), way)
    use((1, -1), (1, 1), (0, 2), (2, 0))
    for x in (-1, 1):
        recv(A0, (x, 2), "z+")
        recv(A1, (x, 2), "z-")
        use((x, 2))
    for z in (-1, 1):
        recv(B0, (2, z), "x+")
        recv(B1, (2, z), "x-")
        use((2, z))
    recv(A0, (2, 2), "z+")
    recv(A1, (2, 2), "z-")
    recv(B0, (2, 2), "x+")
    recv(B1, (2, 2), "x-")
    use((2, 2))
    return plan


def greet(others):
    barrier = pltpu.get_barrier_semaphore()
    for other in others:
        pl.semaphore_signal(barrier, inc=1, device_id=other, device_id_type=MESH)
    pl.semaphore_wait(barrier, len(others))


def step_kernel(
    plan,
    found,
    t_ref,
    panel_ref,
    contrast_ref,
    weight_ref,
    w_hbm,
    fs_ref,
    fa_ref,
    mirror_ref,
    out_ref,
    held,
    prod,
    mate_out,
    mate_in,
    sums,
    y_in,
    z_out,
    s_in,
    b_out,
    b_in,
    t_pad,
    w_ref,
    cw_ref,
    lat,
    spec,
    w_sem,
    ring_send,
    ring_recv,
    mate_send,
    mate_recv,
    y_send,
    y_recv,
    z_send,
    z_recv,
    b_send,
    b_recv,
):
    row = lax.axis_index("row")
    col = lax.axis_index("col")
    x, z = row // NZ, row % NZ
    y, core = col // 2, col % 2
    f32, bf16 = jnp.float32, jnp.bfloat16

    def block_of(rel):
        return ((x + rel[0] + NX) % NX) * NZ + (z + rel[1] + NZ) % NZ

    table_copy = pltpu.make_async_copy(w_hbm, w_ref, w_sem)
    table_copy.start()
    for first in range(ITERS):
        held[first, row, 2 * HALF - 16 :] = jnp.zeros((16, 128), bf16)
    held[0, row, : 2 * BLK] = panel_ref[...]
    greet(
        [{"row": (row + k) % ROWS} for k in range(1, ROWS)]
        + [{"col": (col + k) % COLS} for k in range(1, COLS)]
    )
    mate = {"col": y * 2 + (1 - core)}
    y_peers = [{"col": ((y + k) % NY) * 2 + core} for k in range(1, NY)]

    slot = {}
    for event in plan:
        if event[0] == "send":
            slot[event[1:]] = len(slot)
    order = [event[1] for event in plan if event[0] == "use"]

    def ring_copy(it, part, rel, way, number):
        here = held.at[it, block_of(rel), pl.ds(part[0], part[1])]
        return pltpu.make_async_remote_copy(
            src_ref=here,
            dst_ref=here,
            send_sem=ring_send.at[number],
            recv_sem=ring_recv.at[it, number],
            device_id={"row": block_of(STEP[way])},
            device_id_type=MESH,
        )

    def mate_copy(it, s):
        return pltpu.make_async_remote_copy(
            src_ref=mate_out.at[s],
            dst_ref=mate_in.at[it, s],
            send_sem=mate_send.at[s],
            recv_sem=mate_recv.at[it, s],
            device_id=mate,
            device_id_type=MESH,
        )

    def y_copy(it, s, k):
        to = (y + k) % NY
        number = s * 3 + k - 1
        return pltpu.make_async_remote_copy(
            src_ref=sums.at[s, pl.ds(pl.multiple_of(to * PER, PER), PER)],
            dst_ref=y_in.at[it, s, k - 1],
            send_sem=y_send.at[number],
            recv_sem=y_recv.at[it, number],
            device_id=y_peers[k - 1],
            device_id_type=MESH,
        )

    def z_copy(it, s):
        return pltpu.make_async_remote_copy(
            src_ref=z_out.at[s],
            dst_ref=s_in.at[it, row],
            send_sem=z_send.at[s],
            recv_sem=z_recv.at[it, s],
            device_id={"row": block_of(order[s])},
            device_id_type=MESH,
        )

    def z_arrival(it, s):
        back = (-order[s][0], -order[s][1])
        return pltpu.make_async_remote_copy(
            src_ref=z_out.at[s],
            dst_ref=s_in.at[it, block_of(back)],
            send_sem=z_send.at[s],
            recv_sem=z_recv.at[it, s],
            device_id={"row": block_of(back)},
            device_id_type=MESH,
        )

    def b_copy(it, k):
        return pltpu.make_async_remote_copy(
            src_ref=b_out.at[pl.ds(2 * k, 2)],
            dst_ref=b_in.at[it, core * NY + y],
            send_sem=b_send.at[k],
            recv_sem=b_recv.at[it, col],
            device_id={"col": k},
            device_id_type=MESH,
        )

    def b_arrival(it, k):
        return pltpu.make_async_remote_copy(
            src_ref=b_out.at[pl.ds(2 * k, 2)],
            dst_ref=b_in.at[it, k % 2 * NY + k // 2],
            send_sem=b_send.at[k],
            recv_sem=b_recv.at[it, k],
            device_id={"col": k},
            device_id_type=MESH,
        )

    def multiply(it, s, rel):
        block = block_of(rel)
        here = s % 4
        for chunk in range(LANES // 256):
            rows = slice(chunk * 256, (chunk + 1) * 256)
            prod[here, :, rows] = dot(t_pad[rows, : 2 * HALF], held[it, block]).T
        start = pl.multiple_of((1 - core) * 64, 64)
        mate_out[s] = prod[here, pl.ds(start, 64), :].astype(bf16)
        mate_copy(it, s).start()

    def add_mate(it, s):
        mate_copy(it, s).wait_recv()
        start = pl.multiple_of(core * 64, 64)
        sums[s] = (prod[s % 4, pl.ds(start, 64), :] + mate_in[it, s].astype(f32)).astype(bf16)
        for k in (2, 1, 3):
            y_copy(it, s, k).start()

    def add_y(it, s):
        total = sums[s, pl.ds(pl.multiple_of(y * PER, PER), PER)].astype(f32)
        for k in range(1, NY):
            y_copy(it, s, k).wait_recv()
            total += y_in[it, s, k - 1].astype(f32)
        if s == 0:
            s_in[it, row] = total.astype(bf16)
        else:
            z_out[s] = total.astype(bf16)
            z_copy(it, s).start()

    def prepare():
        for part in range(3):
            turned = contrast_ref[part].T * weight_ref[:, :NT]
            turned = jnp.concatenate([turned, jnp.zeros((NP, TPAD - NT), f32)], axis=1)
            high, rest = turned.astype(bf16), turned
            pieces = []
            for _ in range(3):
                pieces.append(high)
                rest = rest - high.astype(f32)
                high = rest.astype(bf16)
            for side in range(2):
                picked = [dot(mirror_ref[side], piece) for piece in pieces]
                cw_ref[side, part] = picked[0] + picked[1] + picked[2]
        for first in (LDEG + 1, QH + LDEG):
            lat[:, first * CS : (QH if first < QH else QPAD) * CS, :] = jnp.zeros(
                (2, ((QH if first < QH else QPAD) - first) * CS, 128), f32
            )

    def pad_t():
        t_pad[656:, :] = jnp.zeros((LANES - 656, KPAD), bf16)
        t_pad[:, KPAD - 128 :] = jnp.zeros((LANES, 128), bf16)
        t_pad[:BLK, : 2 * BLK] = t_ref[...]

    def iteration(it, carry):
        s = 0
        for event in plan:
            if event[0] == "send":
                _, part, rel, way = event
                ring_copy(it, part, rel, way, slot[event[1:]]).start()
            elif event[0] == "recv":
                _, part, rel, way = event
                there = ((rel[0] + STEP[way][0]) % NX, (rel[1] + STEP[way][1]) % NZ)
                ring_copy(it, part, rel, way, slot[(part, there, way)]).wait_recv()
            else:
                if s == 0:
                    pl.when(it == 0)(pad_t)
                multiply(it, s, event[1])
                if s == 0:
                    pl.when(it == 0)(prepare)
                if s >= 3:
                    add_mate(it, s - 3)
                if s >= 7:
                    add_y(it, s - 7)
                s += 1
        add_mate(it, ROWS - 3)
        add_mate(it, ROWS - 2)
        add_y(it, ROWS - 7)
        add_mate(it, ROWS - 1)
        for late in range(ROWS - 6, ROWS):
            add_y(it, late)
        pl.when(it == 0)(table_copy.wait)
        for s in range(1, ROWS):
            z_arrival(it, s).wait_recv()

        def coefficients(block, window):
            lanes = slice(window * 128, (window + 1) * 128)
            return jnp.concatenate([s_in[it, block, :, lanes], s_in[it, block + 8, :, lanes]], axis=0)

        legendre_in(found, coefficients, w_ref, lat)
        columns(fs_ref, fa_ref, cw_ref, lat, spec)

        def done(k):
            @pl.when(col != k)
            def _():
                b_copy(it, k).start()

        legendre_out(found, w_ref, spec, b_out, done)
        b_in[it, core * NY + y] = b_out[pl.ds(2 * col, 2)]
        for event in plan:
            if event[0] == "send":
                _, part, rel, way = event
                ring_copy(it, part, rel, way, slot[event[1:]]).wait_send()
        for s in range(ROWS):
            mate_copy(it, s).wait_send()
            for k in range(1, NY):
                y_copy(it, s, k).wait_send()
            if s > 0:
                z_copy(it, s).wait_send()
        for k in range(COLS):

            @pl.when(col != k)
            def _():
                b_arrival(it, k).wait_recv()

        parts = []
        for half in range(2):
            value = jnp.concatenate([b_in[it, k, half].astype(f32) for k in range(COLS)], axis=0)
            parts.append(value.T[:BLK])
        value = (jnp.concatenate(parts, axis=0) + panel_ref[...].astype(f32)).astype(bf16)

        @pl.when(it == 0)
        def _():
            held[1, row, : 2 * BLK] = value

        @pl.when(it == 1)
        def _():
            out_ref[...] = value

        for k in range(COLS):

            @pl.when(col != k)
            def _():
                b_copy(it, k).wait_send()

        return carry

    lax.fori_loop(0, ITERS, iteration, 0)


def steps(t, panel, contrast, weight, w, fs, fa, mirror, found):
    plan = ring_plan()
    sends = sum(event[0] == "send" for event in plan)
    vmem = pl.BlockSpec(memory_space=pltpu.VMEM)
    dma = pltpu.SemaphoreType.DMA
    bf16, f32 = jnp.bfloat16, jnp.float32
    return pl.pallas_call(
        functools.partial(step_kernel, plan, found),
        out_shape=jax.ShapeDtypeStruct((2 * BLK, 128), bf16),
        in_specs=[vmem] * 4 + [pl.BlockSpec(memory_space=pl.ANY)] + [vmem] * 3,
        out_specs=vmem,
        scratch_shapes=[
            pltpu.VMEM((ITERS, ROWS, 2 * HALF, 128), bf16),
            pltpu.VMEM((4, 128, LANES), f32),
            pltpu.VMEM((ROWS, 64, LANES), bf16),
            pltpu.VMEM((ITERS, ROWS, 64, LANES), bf16),
            pltpu.VMEM((ROWS, 64, LANES), bf16),
            pltpu.VMEM((ITERS, ROWS, NY - 1, PER, LANES), bf16),
            pltpu.VMEM((ROWS, PER, LANES), bf16),
            pltpu.VMEM((ITERS, ROWS, PER, LANES), bf16),
            pltpu.VMEM((ROWS, PER, LANES), bf16),
            pltpu.VMEM((ITERS, COLS, 2, PER, LANES), bf16),
            pltpu.VMEM((LANES, KPAD), bf16),
            pltpu.VMEM(w.shape, bf16),
            pltpu.VMEM((2, 3, PH, TPAD), f32),
            pltpu.VMEM((2, QPAD * CS, 128), f32),
            pltpu.VMEM((2, QPAD * CS, 128), f32),
            dma(()),
            dma((sends,)),
            dma((ITERS, sends)),
            dma((ROWS,)),
            dma((ITERS, ROWS)),
            dma((ROWS * 3,)),
            dma((ITERS, ROWS * 3)),
            dma((ROWS,)),
            dma((ITERS, ROWS)),
            dma((COLS,)),
            dma((ITERS, COLS)),
        ],
        compiler_params=pltpu.CompilerParams(
            collective_id=0, has_side_effects=True, vmem_limit_bytes=58 * MIB
        ),
        name="steps",
    )(t, panel, contrast, weight, w, fs, fa, mirror)


def body(tmatrix, panel, contrast):
    found, windows, fs, fa, mirror, weight = tables()
    weight = jnp.asarray(np.pad(weight, (0, TPAD - NT)).reshape(1, TPAD))
    return steps(
        tmatrix,
        panel,
        contrast,
        weight,
        jnp.asarray(windows),
        jnp.asarray(fs),
        jnp.asarray(fa),
        jnp.asarray(mirror),
        found,
    )


def solution(mesh):
    placed = (P("row", "col"), P("col", "row"), P())
    return jax.shard_map(
        body, mesh=mesh, in_specs=placed, out_specs=P("col", "row"), check_vma=False
    )
```
